512 devices in a mesh: row: 16 (over z_lo, x), col: 32 (over z_hi, y, core).
Axes of the slice: x: 4, y: 4, z: 16 (z_hi: 4, z_lo: 4; z = z_hi * 4 + z_lo), core: 2. Of those that a mesh axis runs over, the one named last changes fastest.
Arguments:
- coeffs: float32 [8192, 8192], P('row', 'col'), may hold values from -6 to 6
- diag_energy: float32 [8192, 8192], P('row', 'col'), may hold values from 1 to 9
- energy: float32 [1], replicated, may hold values from 4 to 6
- h_blocks: bfloat16 [64, 24, 128, 128], P('row'), may hold values from -0.109375 to 0.109375
- pattern: int32 [64, 24], replicated, may hold values from 0 to 63, as said below
- counts: int32 [64], replicated, may hold values from 1 to 24, 960 in all
Outputs:
- correction: float32 [8192, 8192], P('row', 'col')
The draws below stay inside these ranges and needn't reach their ends.
Inputs may be any that keep to these rules, and one draw needn't show every extreme that they name: `pattern`: each row lists 24 different block indices; block columns q * 2 to q * 2 + 1 form group q, and block c * 2 to c * 2 + 1 form the blocks of group c; all slots of the rows of one group together name exactly half of the blocks of every group.
All inputs are finite; a program needn't handle non-finite values.
Results may differ from the reference program's by a relative error of at most 0.0018.
Values may be sent and summed in bfloat16 or wider, within the bound.
No kernel may reach another device: no remote copies, remote signals or barrier semaphores. Data moves between devices by JAX's collectives and lax.ppermute only.
A program may use at most 128 MiB of HBM per device.

```python
import math
import jax
import jax.numpy as jnp
import numpy as np
from jax import lax

STRINGS = 8192
BLK = 128
NNZ = 24
NBLK = 64
CB = 2


def draw_pattern(key, part):
    key = jax.random.fold_in(key, 7)
    pick_key, order_key, slot_key = jax.random.split(key, 3)
    groups = NBLK // CB
    halfway = NBLK // 2
    pick_scores = jax.random.randint(pick_key, (groups, groups, CB), 0, 1048576) * CB + jnp.arange(CB, dtype=jnp.int32)
    chosen = jnp.argsort(pick_scores, axis=-1)[:, :, :CB // 2].astype(jnp.int32)
    owners = jnp.arange(groups, dtype=jnp.int32)[None, :, None] * CB
    allowed = (owners + chosen).reshape(groups, halfway)
    order_scores = jax.random.randint(order_key, (groups, halfway), 0, 1048576) * halfway + jnp.arange(halfway, dtype=jnp.int32)[None, :]
    allowed = jnp.take_along_axis(allowed, jnp.argsort(order_scores, axis=-1).astype(jnp.int32), axis=-1)
    stride = halfway - NNZ
    window = (jnp.arange(CB, dtype=jnp.int32)[:, None] * stride + jnp.arange(NNZ, dtype=jnp.int32)[None, :]) % halfway
    rows_all = allowed[:, window]
    slot_scores = jax.random.randint(slot_key, (groups, CB, NNZ), 0, 1048576) * NNZ + jnp.arange(NNZ, dtype=jnp.int32)
    rows_all = jnp.take_along_axis(rows_all, jnp.argsort(slot_scores, axis=-1).astype(jnp.int32), axis=-1)
    return rows_all.reshape(NBLK, NNZ).astype(jnp.int32)


def steps_of(own_key, extent, cuts, smallest, high):
    loudness, own = 1.0, jax.random.fold_in(own_key, 6)
    for position, parts in cuts:
        draws = jnp.exp(jax.random.uniform(jax.random.fold_in(own, position), (parts,), jnp.float32, smallest / len(cuts), high / len(cuts)))
        loudness = loudness * jnp.repeat(draws, extent[position] // parts).reshape([-1 if axis == position else 1 for axis in range(len(extent))])
    return loudness


def length_profile(number_of, total, limit, skew):
    portions = [(1 << 20) // math.isqrt(rank ** skew) + 1 for rank in range(2, number_of + 1)]
    spare, given = total - limit - (number_of - 1), [1] * (number_of - 1)
    while spare > 0:
        movable = [i for i in range(number_of - 1) if given[i] < limit]
        mass, budget = sum([portions[i] for i in movable]), spare
        for i in movable:
            addition = min(limit - given[i], max(1, budget * portions[i] // mass), spare)
            given[i] = given[i] + addition
            spare = spare - addition
    return np.array([limit] + given)


def ragged(rng, count, total, limit, lean):
    if count == 2:
        one = jax.random.randint(rng, (), max(1, total - limit), min(limit, total - 1) + 1)
        return jnp.stack([one, total - one])
    tallies = jnp.asarray(length_profile(count, total, limit, lean), jnp.int32)
    twos = (count - 1) // 2
    donor, receiver = tallies[1:1 + 2 * twos:2], tallies[2:2 + 2 * twos:2]
    slack = jnp.minimum(donor - 1, limit - receiver)
    shifted = jax.random.randint(jax.random.fold_in(rng, 1), (twos,), 0, 1 << 20) % (slack + 1)
    tallies = tallies.at[1:1 + 2 * twos:2].set(donor - shifted).at[2:2 + 2 * twos:2].set(receiver + shifted)
    return tallies[jax.random.permutation(jax.random.fold_in(rng, 2), count)]


def noise(rng, shape, spread, limit, pieces=(), kind=jnp.bfloat16):
    values = jax.random.normal(rng, shape, jnp.float32) * spread
    if len(pieces) > 0:
        values = steps_of(rng, shape, pieces, -0.22, 0.18) * values
    return jnp.clip(values, min=-limit, max=limit).astype(kind)


def setup_inputs(seed: int = 0) -> dict:
    splits = jax.random.split(jax.random.key(seed), 7)
    coeffs = noise(splits[0], (STRINGS, STRINGS), 1.0, 6.0, ((0, 16), (1, 32)), jnp.float32)
    diag_energy = jnp.clip(1.0 + 8.0 * jax.random.uniform(splits[1], (STRINGS, STRINGS), jnp.float32) ** steps_of(splits[1], (STRINGS, STRINGS), ((0, 16), (1, 32)), -0.2, 0.2), 1.0, 9.0)
    energy = jnp.clip(jax.random.uniform(splits[2], (1,), jnp.float32, 4.0, 6.0), 4.0, 6.0)
    h_blocks = noise(splits[3], (NBLK, NNZ, BLK, BLK), (NNZ * BLK) ** -0.5, 0.109375, ((0, 16),))
    pattern = draw_pattern(jax.random.fold_in(splits[6], 71), 0)
    counts = ragged(splits[5], NBLK, NBLK * NNZ * 5 // 8, NNZ, 2).astype(jnp.int32)
    return {"coeffs": coeffs, "diag_energy": diag_energy, "energy": energy, "h_blocks": h_blocks, "pattern": pattern, "counts": counts}


def reference(coeffs, diag_energy, energy, h_blocks, pattern, counts):
    coeff_half = coeffs.astype(jnp.bfloat16)
    filled = jnp.arange(NNZ, dtype=jnp.int32)[None, :] < counts[:, None]
    h_live = jnp.where(filled[:, :, None, None], h_blocks, jnp.zeros_like(h_blocks))
    by_cols = coeff_half.reshape(STRINGS, NBLK, BLK)
    by_rows = coeff_half.reshape(NBLK, BLK, STRINGS)

    def column_term(column):
        picked = by_cols[:, pattern[column]]
        return jnp.einsum("rsk,ski->ri", picked.astype(jnp.float32), h_live[column].astype(jnp.float32))

    def row_term(column):
        picked = by_rows[pattern[column]]
        return jnp.einsum("skc,ski->ic", picked.astype(jnp.float32), h_live[column].astype(jnp.float32))

    indices = jnp.arange(NBLK, dtype=jnp.int32)
    direct_term = lax.map(column_term, indices)
    direct_term = jnp.transpose(direct_term, (1, 0, 2)).reshape(STRINGS, STRINGS)
    mirror_term = lax.map(row_term, indices).reshape(STRINGS, STRINGS)
    sigma_full = direct_term + mirror_term + diag_energy * coeffs
    shift_value = energy[0]
    return (sigma_full - shift_value * coeffs) / jnp.maximum(jnp.abs(diag_energy - shift_value), 1.0)
```

```python
import functools

import jax
import jax.numpy as jnp
from jax import lax
from jax.experimental import pallas as pl
from jax.experimental.pallas import tpu as pltpu
from jax.sharding import Mesh, PartitionSpec as P

AXES = ("zl", "x", "zh", "y", "co")
ROW = ("zl", "x")
COL = ("zh", "y", "co")
W = 128
VMEM_LIMIT = 56 * 1024 * 1024


def shifted(value, axis, step):
    return lax.ppermute(value, axis, [(i, (i + step) % 4) for i in range(4)])


def swap_cores(value):
    return lax.ppermute(value, "co", [(0, 1), (1, 0)])


def panel_direct_kernel(pos, own_ref, other_ref, out_ref):
    out_ref[...] = jnp.zeros_like(out_ref)
    cols = own_ref.shape[0]
    for part, h_ref in enumerate((own_ref, other_ref)):
        for m in range(cols):
            column = part * cols + m

            def place(s, carry, h_ref=h_ref, m=m, column=column):
                at = pos[column, s]

                @pl.when(at >= 0)
                def _():
                    rows = pl.ds(pl.multiple_of(at * W, W), W)
                    out_ref[rows, column * W : (column + 1) * W] = h_ref[m, s]

                return carry

            lax.fori_loop(0, h_ref.shape[1], place, 0)


def panel_direct(pos, own, other):
    return pl.pallas_call(
        panel_direct_kernel,
        out_shape=jax.ShapeDtypeStruct((4096, 512), jnp.bfloat16),
        in_specs=[
            pl.BlockSpec(memory_space=pltpu.SMEM),
            pl.BlockSpec(memory_space=pltpu.VMEM),
            pl.BlockSpec(memory_space=pltpu.VMEM),
        ],
        out_specs=pl.BlockSpec(memory_space=pltpu.VMEM),
        compiler_params=pltpu.CompilerParams(vmem_limit_bytes=VMEM_LIMIT),
        name="panel_direct",
    )(pos, own, other)


def panel_mirror_kernel(pos, h_ref, out_ref):
    out_ref[...] = jnp.zeros_like(out_ref)
    for m in range(h_ref.shape[0]):

        def place(s, carry, m=m):
            at = pos[m, s]

            @pl.when(at >= 0)
            def _():
                lanes = pl.ds(pl.multiple_of(at * W, W), W)
                out_ref[m * W : (m + 1) * W, lanes] = h_ref[m, s].T

            return carry

        lax.fori_loop(0, h_ref.shape[1], place, 0)


def panel_mirror(pos, h):
    return pl.pallas_call(
        panel_mirror_kernel,
        out_shape=jax.ShapeDtypeStruct((512, 8192), jnp.bfloat16),
        in_specs=[
            pl.BlockSpec(memory_space=pltpu.SMEM),
            pl.BlockSpec(memory_space=pltpu.VMEM),
        ],
        out_specs=pl.BlockSpec(memory_space=pltpu.VMEM),
        compiler_params=pltpu.CompilerParams(vmem_limit_bytes=VMEM_LIMIT),
        name="panel_mirror",
    )(pos, h)


def direct_kernel(places, *refs):
    panel_ref, out_ref = refs[-2], refs[-1]
    total = None
    for where, ref in zip(places, refs[:-2]):
        for t, place in enumerate(where):
            term = jnp.dot(
                ref[t], panel_ref[place * 256 : (place + 1) * 256, :], preferred_element_type=jnp.float32
            )
            total = term if total is None else total + term
    out_ref[...] = total


def direct_part(places, arrays, panel):
    return pl.pallas_call(
        functools.partial(direct_kernel, places),
        out_shape=jax.ShapeDtypeStruct((512, 512), jnp.float32),
        in_specs=[pl.BlockSpec(memory_space=pltpu.VMEM)] * (len(arrays) + 1),
        out_specs=pl.BlockSpec(memory_space=pltpu.VMEM),
        compiler_params=pltpu.CompilerParams(vmem_limit_bytes=VMEM_LIMIT),
        name="direct_part",
    )(*arrays, panel)


def mirror_kernel(places, *refs):
    panel_ref, out_ref = refs[-2], refs[-1]
    total = None
    for where, ref in zip(places, refs[:-2]):
        for t, place in enumerate(where):
            term = jnp.dot(
                panel_ref[:, place * 512 : (place + 1) * 512], ref[t], preferred_element_type=jnp.float32
            )
            total = term if total is None else total + term
    out_ref[...] = total


def mirror_part(places, arrays, panel):
    return pl.pallas_call(
        functools.partial(mirror_kernel, places),
        out_shape=jax.ShapeDtypeStruct((512, 256), jnp.float32),
        in_specs=[pl.BlockSpec(memory_space=pltpu.VMEM)] * (len(arrays) + 1),
        out_specs=pl.BlockSpec(memory_space=pltpu.VMEM),
        compiler_params=pltpu.CompilerParams(vmem_limit_bytes=VMEM_LIMIT),
        name="mirror_part",
    )(*arrays, panel)


def on_device(coeffs, diag_energy, energy, h_blocks, pattern, counts):
    zl, x, zh, y, co = (lax.axis_index(a) for a in AXES)
    row_id = zl * 4 + x
    chip_col = zh * 4 + y
    slots = h_blocks.shape[1]

    half = coeffs.astype(jnp.bfloat16)[None]

    flat = h_blocks.reshape(2, 2 * slots, W, W)
    piece = lax.dynamic_slice(flat, (co, chip_col * 3, 0, 0), (1, 3, W, W))[0]
    turn = [((r * 16 + k) * 2 + c, (k * 16 + r) * 2 + c) for r in range(16) for k in range(16) for c in range(2)]
    piece = lax.ppermute(piece, AXES, turn)
    h_own = lax.all_gather(piece, ROW, axis=0, tiled=True).reshape(2, slots, W, W)
    h_other = swap_cores(h_own)

    filled = jnp.arange(slots, dtype=jnp.int32)[None, :] < counts[:, None]

    blk = lax.dynamic_slice_in_dim(pattern, chip_col * 4, 4, 0)
    live = lax.dynamic_slice_in_dim(filled, chip_col * 4, 4, 0)
    group = blk // 2
    at = (((zh - group // 8) % 4) * 4 + (y - (group // 2) % 4) % 4) * 2 + blk % 2
    at = jnp.where(live & (group % 2 == co), at, -1)
    pos_direct = jnp.where(co == 0, at, jnp.concatenate([at[2:], at[:2]], axis=0))

    blk = lax.dynamic_slice_in_dim(pattern, row_id * 4, 4, 0)
    live = lax.dynamic_slice_in_dim(filled, row_id * 4, 4, 0)
    owner = blk // 4
    at = (((zl - owner // 4) % 4) * 4 + (x - owner % 4) % 4) * 4 + blk % 4
    pos_mirror = jnp.where(live, at, -1)

    panel_m = panel_mirror(pos_mirror, h_blocks)
    panel_d = panel_direct(pos_direct, h_own, h_other)

    zh1, zh3 = shifted(half, "zh", 1), shifted(half, "zh", 3)
    zl_tiles = [shifted(half, "zl", d) for d in (1, 2, 3)]
    zh2 = shifted(half, "zh", 2)
    y0 = [half] + [shifted(half, "y", d) for d in (1, 2, 3)]
    x0 = [half] + [shifted(half, "x", d) for d in (1, 2, 3)]
    near = jnp.concatenate([zh1, zh3], axis=0)
    y13 = [near] + [shifted(near, "y", d) for d in (1, 2, 3)]
    mine = jnp.concatenate(zl_tiles, axis=0)
    x123 = [mine] + [shifted(mine, "x", d) for d in (1, 2, 3)]
    y2 = [zh2] + [shifted(zh2, "y", d) for d in (1, 2, 3)]

    mirror = mirror_part([(d,) for d in range(4)], x0, panel_m)
    direct = direct_part([(d,) for d in range(4)], y0, panel_d)
    direct = direct + direct_part([(4 + d, 12 + d) for d in range(4)], y13, panel_d)
    mirror = mirror + mirror_part([(4 + d, 8 + d, 12 + d) for d in range(4)], x123, panel_m)
    direct = direct + direct_part([(8 + d,) for d in range(4)], y2, panel_d)
    direct_term = direct[:, :256] + swap_cores(direct[:, 256:])
    sigma_full = direct_term + mirror + diag_energy * coeffs
    shift_value = energy[0]
    return (sigma_full - shift_value * coeffs) / jnp.maximum(jnp.abs(diag_energy - shift_value), 1.0)


def solution(mesh):
    fine = Mesh(mesh.devices.reshape(4, 4, 4, 4, 2), AXES)
    placed = (P(ROW, COL), P(ROW, COL), P(), P(ROW, None, None, None), P(), P())
    return jax.shard_map(on_device, mesh=fine, in_specs=placed, out_specs=P(ROW, COL), check_vma=False)
```

```python
import jax
import jax.numpy as jnp
from jax import lax
from jax.experimental import pallas as pl
from jax.experimental.pallas import tpu as pltpu
from jax.sharding import Mesh, PartitionSpec as P

AXES = ("zl", "x", "zh", "y", "co")
ROW = ("zl", "x")
COL = ("zh", "y", "co")
W = 128
VMEM_LIMIT = 56 * 1024 * 1024
PARAMS = pltpu.CompilerParams(vmem_limit_bytes=VMEM_LIMIT)


def shifted(value, axis, step):
    return lax.ppermute(value, axis, [(i, (i + step) % 4) for i in range(4)])


def swap_cores(value):
    return lax.ppermute(value, "co", [(0, 1), (1, 0)])


def turned(value, cross):
    pairs = [
        ((r * 16 + k) * 2 + c, (k * 16 + r) * 2 + (c ^ cross))
        for r in range(16)
        for k in range(16)
        for c in range(2)
    ]
    return lax.ppermute(value, AXES, pairs)


def pack_kernel(pos, co, h_ref, out_ref):
    out_ref[...] = jnp.zeros_like(out_ref)
    for m in range(2):

        def place(s, carry, m=m):
            at = pos[m, s]

            @pl.when(at >= 0)
            def _():
                out_ref[at, :, m * W : (m + 1) * W] = h_ref[m, s]

            return carry

        lax.fori_loop(0, h_ref.shape[1], place, 0)


def pack(pos, co, h_blocks):
    slots = h_blocks.shape[1]
    return pl.pallas_call(
        pack_kernel,
        out_shape=jax.ShapeDtypeStruct((32, W, 2 * W), jnp.bfloat16),
        grid_spec=pltpu.PrefetchScalarGridSpec(
            num_scalar_prefetch=2,
            grid=(1,),
            in_specs=[pl.BlockSpec((2, slots, W, W), lambda i, pos, co: (co[0], 0, 0, 0))],
            out_specs=pl.BlockSpec((32, W, 2 * W), lambda i, pos, co: (0, 0, 0)),
        ),
        compiler_params=PARAMS,
        name="pack",
    )(pos, co, h_blocks)


def gathered(where, bits, tiles, h_ref, column, pair, take):
    zl = where[0]
    strings, blocks = [], []
    for d, tile in enumerate(tiles):
        owner = lax.rem(zl - d + 4, 4)
        for j in range(2):
            i = owner * 2 + j
            start = pl.multiple_of((2 * j + bits[pair, i]) * W, W)
            strings.append(take(tile, start))
            blocks.append(h_ref[column, i])
    return strings, jnp.concatenate(blocks, axis=0)


def direct_kernel(where, bits, t0, t1, t2, t3, own_ref, other_ref, out_ref, kept_ref):
    for column in range(4):
        for h_ref, half in ((own_ref, where[2]), (other_ref, 1 - where[2])):
            strings, blocks = gathered(
                where,
                bits,
                (t0, t1, t2, t3),
                h_ref,
                column,
                column * 2 + half,
                lambda tile, start: tile[:, pl.ds(start, W)],
            )
            part = jnp.dot(jnp.concatenate(strings, axis=1), blocks, preferred_element_type=jnp.float32)
            lanes = pl.ds(pl.multiple_of(half * 2 * W, 2 * W), 2 * W)
            out_ref[column, :, lanes] = part.astype(jnp.bfloat16)

            @pl.when(where[1] == column)
            def _():
                kept_ref[:, lanes] = part


def mirror_kernel(where, bits, t0, t1, t2, t3, own_ref, other_ref, out_ref, kept_ref):
    for column in range(4):
        for h_ref, half in ((own_ref, where[2]), (other_ref, 1 - where[2])):
            strings, blocks = gathered(
                where,
                bits,
                (t0, t1, t2, t3),
                h_ref,
                column,
                column * 2 + half,
                lambda tile, start: tile[pl.ds(start, W), :],
            )
            part = lax.dot_general(
                blocks,
                jnp.concatenate(strings, axis=0),
                (((0,), (0,)), ((), ())),
                preferred_element_type=jnp.float32,
            )
            rows = pl.ds(pl.multiple_of(half * 2 * W, 2 * W), 2 * W)
            out_ref[column, rows, :] = part.astype(jnp.bfloat16)

            @pl.when(where[1] == column)
            def _():
                kept_ref[rows, :] = part


def partial_sums(kernel, name, where, bits, tiles, own, other):
    shape = tiles[0].shape
    return pl.pallas_call(
        kernel,
        out_shape=(
            jax.ShapeDtypeStruct((4, *shape), jnp.bfloat16),
            jax.ShapeDtypeStruct(shape, jnp.float32),
        ),
        in_specs=[pl.BlockSpec(memory_space=pltpu.SMEM)] * 2 + [pl.BlockSpec(memory_space=pltpu.VMEM)] * 6,
        out_specs=(pl.BlockSpec(memory_space=pltpu.VMEM), pl.BlockSpec(memory_space=pltpu.VMEM)),
        compiler_params=PARAMS,
        name=name,
    )(where, bits, *tiles, own, other)


def summed(parts, kept, x):
    got = lax.all_to_all(parts, "x", 0, 0, tiled=True)
    others = (jnp.arange(4) != x)[:, None, None]
    return kept + jnp.sum(jnp.where(others, got, jnp.zeros_like(got)).astype(jnp.float32), axis=0)


def on_device(coeffs, diag_energy, energy, h_blocks, pattern, counts):
    zl, x, zh, y, co = (lax.axis_index(a).astype(jnp.int32) for a in AXES)
    row_id = zl * 4 + x
    slots = h_blocks.shape[1]

    half = coeffs.astype(jnp.bfloat16)

    first, last = half[:256], half[256:]
    here = turned(jnp.where(co == 0, first, last), 0)
    there = turned(jnp.where(co == 0, last, first), 1)
    tile = jnp.where(
        co == 0, jnp.concatenate([here, there], axis=1), jnp.concatenate([there, here], axis=1)
    )
    direct_tiles = [tile] + [shifted(tile, "zl", d) for d in (1, 2, 3)]
    mirror_tiles = [half] + [shifted(half, "zl", d) for d in (1, 2, 3)]

    filled = jnp.arange(slots, dtype=jnp.int32)[None, :] < counts[:, None]
    begin = row_id * 4 + co * 2
    blk = lax.dynamic_slice_in_dim(pattern, begin, 2, 0)
    live = lax.dynamic_slice_in_dim(filled, begin, 2, 0)
    owner = blk // 4
    at = (owner % 4) * 8 + (owner // 4) * 2 + (blk % 4) // 2
    packed = pack(jnp.where(live, at, -1), co[None], h_blocks)
    own = lax.all_to_all(packed.reshape(4, 8, W, 2 * W), "x", 0, 0, tiled=True)
    other = swap_cores(lax.optimization_barrier((own, tile))[0])

    names = lax.dynamic_slice_in_dim(pattern, zl * 16, 16, 0).reshape(8, 1, 2 * slots)
    i = jnp.arange(8, dtype=jnp.int32)
    odd = (8 * (i // 2) + 2 * x + i % 2) * 2 + 1
    bits = jnp.any(names == odd[None, :, None], axis=2).astype(jnp.int32)
    where = jnp.stack([zl, x, co])

    direct, kept_direct = partial_sums(direct_kernel, "direct", where, bits, direct_tiles, own, other)
    direct = summed(direct, kept_direct, x).astype(jnp.bfloat16)
    left, right = direct[:, :256], direct[:, 256:]
    here = turned(jnp.where(co == 0, left, right), 0)
    there = turned(jnp.where(co == 0, right, left), 1)
    direct_term = jnp.where(
        co == 0, jnp.concatenate([here, there], axis=0), jnp.concatenate([there, here], axis=0)
    ).astype(jnp.float32)

    mirror, kept_mirror = partial_sums(mirror_kernel, "mirror", where, bits, mirror_tiles, own, other)
    mirror_term = summed(mirror, kept_mirror, x)

    sigma_full = direct_term + mirror_term + diag_energy * coeffs
    shift_value = energy[0]
    return (sigma_full - shift_value * coeffs) / jnp.maximum(jnp.abs(diag_energy - shift_value), 1.0)


def solution(mesh):
    fine = Mesh(mesh.devices.reshape(4, 4, 4, 4, 2), AXES)
    placed = (P(ROW, COL), P(ROW, COL), P(), P(ROW, None, None, None), P(), P())
    return jax.shard_map(on_device, mesh=fine, in_specs=placed, out_specs=P(ROW, COL), check_vma=False)
```

```python
import jax
import jax.numpy as jnp
from jax import lax
from jax.experimental import pallas as pl
from jax.experimental.pallas import tpu as pltpu
from jax.sharding import Mesh, PartitionSpec as P

AXES = ("zl", "x", "zh", "y", "co")
ROW = ("zl", "x")
COL = ("zh", "y", "co")
W = 128
VMEM_LIMIT = 56 * 1024 * 1024
PARAMS = pltpu.CompilerParams(vmem_limit_bytes=VMEM_LIMIT)


def shifted(value, axis, step):
    return lax.ppermute(value, axis, [(i, (i + step) % 4) for i in range(4)])


def swap_cores(value):
    return lax.ppermute(value, "co", [(0, 1), (1, 0)])


def turned(value, cross):
    pairs = [
        ((r * 16 + k) * 2 + c, (k * 16 + r) * 2 + (c ^ cross))
        for r in range(16)
        for k in range(16)
        for c in range(2)
    ]
    return lax.ppermute(value, AXES, pairs)


def pack_kernel(pos, co, h_ref, out_ref):
    out_ref[...] = jnp.zeros_like(out_ref)
    for m in range(2):

        def place(s, carry, m=m):
            at = pos[m, s]

            @pl.when(at >= 0)
            def _():
                out_ref[at, :, m * W : (m + 1) * W] = h_ref[m, s]

            return carry

        lax.fori_loop(0, h_ref.shape[1], place, 0)


def pack(pos, co, h_blocks):
    slots = h_blocks.shape[1]
    return pl.pallas_call(
        pack_kernel,
        out_shape=jax.ShapeDtypeStruct((32, W, 2 * W), jnp.bfloat16),
        grid_spec=pltpu.PrefetchScalarGridSpec(
            num_scalar_prefetch=2,
            grid=(1,),
            in_specs=[pl.BlockSpec((2, slots, W, W), lambda i, pos, co: (co[0], 0, 0, 0))],
            out_specs=pl.BlockSpec((32, W, 2 * W), lambda i, pos, co: (0, 0, 0)),
        ),
        compiler_params=PARAMS,
        name="pack",
    )(pos, co, h_blocks)


def strings_and_blocks(where, bits, tiles, h_ref, column, pair, take):
    strings, blocks = [], []
    for d, tile in enumerate(tiles):
        owner = lax.rem(where[0] - d + 4, 4)
        for j in range(2):
            i = owner * 2 + j
            start = pl.multiple_of((2 * j + bits[pair, i]) * W, W)
            strings.append(take(tile, start))
            blocks.append(h_ref[column, i])
    return strings, jnp.concatenate(blocks, axis=0)


def direct_kernel(where, bits, t0, t1, t2, t3, h_ref, out_ref, kept_ref):
    for column in range(4):
        strings, blocks = strings_and_blocks(
            where,
            bits,
            (t0, t1, t2, t3),
            h_ref,
            column,
            column * 2 + where[2],
            lambda tile, start: tile[:, pl.ds(start, W)],
        )
        part = jnp.dot(jnp.concatenate(strings, axis=1), blocks, preferred_element_type=jnp.float32)
        out_ref[column] = part.astype(jnp.bfloat16)

        @pl.when(where[1] == column)
        def _():
            kept_ref[...] = part


def mirror_kernel(where, bits, t0, t1, t2, t3, own_ref, other_ref, out_ref, kept_ref):
    for column in range(4):
        for h_ref, half in ((own_ref, where[2]), (other_ref, 1 - where[2])):
            strings, blocks = strings_and_blocks(
                where,
                bits,
                (t0, t1, t2, t3),
                h_ref,
                column,
                column * 2 + half,
                lambda tile, start: tile[pl.ds(start, W), :],
            )
            part = lax.dot_general(
                blocks,
                jnp.concatenate(strings, axis=0),
                (((0,), (0,)), ((), ())),
                preferred_element_type=jnp.float32,
            )
            rows = pl.ds(pl.multiple_of(half * 2 * W, 2 * W), 2 * W)
            out_ref[column, rows, :] = part.astype(jnp.bfloat16)

            @pl.when(where[1] == column)
            def _():
                kept_ref[rows, :] = part


def partial_sums(kernel, name, shape, where, bits, tiles, *hams):
    return pl.pallas_call(
        kernel,
        out_shape=(
            jax.ShapeDtypeStruct((4, *shape), jnp.bfloat16),
            jax.ShapeDtypeStruct(shape, jnp.float32),
        ),
        in_specs=[pl.BlockSpec(memory_space=pltpu.SMEM)] * 2
        + [pl.BlockSpec(memory_space=pltpu.VMEM)] * (4 + len(hams)),
        out_specs=(pl.BlockSpec(memory_space=pltpu.VMEM), pl.BlockSpec(memory_space=pltpu.VMEM)),
        compiler_params=PARAMS,
        name=name,
    )(where, bits, *tiles, *hams)


def exchanged(parts):
    return lax.all_to_all(parts, "x", 0, 0, tiled=True)


def summed(got, kept, x):
    others = (jnp.arange(4) != x)[:, None, None]
    return kept + jnp.sum(jnp.where(others, got, jnp.zeros_like(got)).astype(jnp.float32), axis=0)


def on_device(coeffs, diag_energy, energy, h_blocks, pattern, counts):
    zl, x, zh, y, co = (lax.axis_index(a).astype(jnp.int32) for a in AXES)
    row_id = zl * 4 + x
    slots = h_blocks.shape[1]

    half = coeffs.astype(jnp.bfloat16)

    first, last = half[:256], half[256:]
    here = turned(jnp.where(co == 0, first, last), 0)
    there = turned(jnp.where(co == 0, last, first), 1)
    tile = jnp.where(
        co == 0, jnp.concatenate([here, there], axis=1), jnp.concatenate([there, here], axis=1)
    )
    mirror_tiles = [half] + [shifted(half, "zl", d) for d in (1, 2, 3)]
    tile = lax.optimization_barrier((tile, *mirror_tiles[1:]))[0]
    direct_tiles = [tile] + [shifted(tile, "zl", d) for d in (1, 2, 3)]

    filled = jnp.arange(slots, dtype=jnp.int32)[None, :] < counts[:, None]
    begin = row_id * 4 + co * 2
    blk = lax.dynamic_slice_in_dim(pattern, begin, 2, 0)
    live = lax.dynamic_slice_in_dim(filled, begin, 2, 0)
    owner = blk // 4
    at = (owner % 4) * 8 + (owner // 4) * 2 + (blk % 4) // 2
    packed = pack(jnp.where(live, at, -1), co[None], h_blocks)
    packed = lax.optimization_barrier((packed, here, there, mirror_tiles[1]))[0]
    own = lax.all_to_all(packed.reshape(4, 8, W, 2 * W), "x", 0, 0, tiled=True)
    other = swap_cores(lax.optimization_barrier((own, *direct_tiles[1:]))[0])

    names = lax.dynamic_slice_in_dim(pattern, zl * 16, 16, 0).reshape(8, 1, 2 * slots)
    i = jnp.arange(8, dtype=jnp.int32)
    odd = (8 * (i // 2) + 2 * x + i % 2) * 2 + 1
    bits = jnp.any(names == odd[None, :, None], axis=2).astype(jnp.int32)
    here_first = jnp.stack([zl, x, co])
    there_first = jnp.stack([zl, x, 1 - co])

    upper, kept_upper = partial_sums(direct_kernel, "direct", (256, 256), here_first, bits, direct_tiles, own)
    got_upper = exchanged(upper)
    direct_tiles[3], upper = lax.optimization_barrier((direct_tiles[3], upper))
    lower, kept_lower = partial_sums(direct_kernel, "direct", (256, 256), there_first, bits, direct_tiles, other)
    lower, got_upper = lax.optimization_barrier((lower, got_upper))
    got_lower = exchanged(lower)
    mirror_tiles[3], lower = lax.optimization_barrier((mirror_tiles[3], lower))
    mirror, kept = partial_sums(
        mirror_kernel, "mirror", (512, 256), here_first, bits, mirror_tiles, own, other
    )
    here = turned(summed(got_upper, kept_upper, x).astype(jnp.bfloat16), 0)
    got_lower, mirror = lax.optimization_barrier((got_lower, mirror))
    there = turned(summed(got_lower, kept_lower, x).astype(jnp.bfloat16), 1)
    mirror_term = summed(exchanged(mirror), kept, x)
    direct_term = jnp.where(
        co == 0, jnp.concatenate([here, there], axis=0), jnp.concatenate([there, here], axis=0)
    ).astype(jnp.float32)

    sigma_full = direct_term + mirror_term + diag_energy * coeffs
    shift_value = energy[0]
    return (sigma_full - shift_value * coeffs) / jnp.maximum(jnp.abs(diag_energy - shift_value), 1.0)


def solution(mesh):
    fine = Mesh(mesh.devices.reshape(4, 4, 4, 4, 2), AXES)
    placed = (P(ROW, COL), P(ROW, COL), P(), P(ROW, None, None, None), P(), P())
    return jax.shard_map(on_device, mesh=fine, in_specs=placed, out_specs=P(ROW, COL), check_vma=False)
```

```python
import jax
import jax.numpy as jnp
from jax import lax
from jax.experimental import pallas as pl
from jax.experimental.pallas import tpu as pltpu
from jax.sharding import Mesh, PartitionSpec as P

AXES = ("zl", "x", "zh", "y", "co")
ROW = ("zl", "x")
COL = ("zh", "y", "co")
W = 128
VMEM_LIMIT = 56 * 1024 * 1024
PARAMS = pltpu.CompilerParams(vmem_limit_bytes=VMEM_LIMIT)


def shifted(value, axis, step):
    return lax.ppermute(value, axis, [(i, (i + step) % 4) for i in range(4)])


def swap_cores(value):
    return lax.ppermute(value, "co", [(0, 1), (1, 0)])


def turned(value, cross):
    pairs = [
        ((r * 16 + k) * 2 + c, (k * 16 + r) * 2 + (c ^ cross))
        for r in range(16)
        for k in range(16)
        for c in range(2)
    ]
    return lax.ppermute(value, AXES, pairs)


def pack_kernel(pos, co, h_ref, out_ref):
    out_ref[...] = jnp.zeros_like(out_ref)
    for m in range(2):

        def place(s, carry, m=m):
            at = pos[m, s]

            @pl.when(at >= 0)
            def _():
                out_ref[at, :, m * W : (m + 1) * W] = h_ref[m, s]

            return carry

        lax.fori_loop(0, h_ref.shape[1], place, 0)


def pack(pos, co, h_blocks):
    slots = h_blocks.shape[1]
    return pl.pallas_call(
        pack_kernel,
        out_shape=jax.ShapeDtypeStruct((32, W, 2 * W), jnp.bfloat16),
        grid_spec=pltpu.PrefetchScalarGridSpec(
            num_scalar_prefetch=2,
            grid=(1,),
            in_specs=[pl.BlockSpec((2, slots, W, W), lambda i, pos, co: (co[0], 0, 0, 0))],
            out_specs=pl.BlockSpec((32, W, 2 * W), lambda i, pos, co: (0, 0, 0)),
        ),
        compiler_params=PARAMS,
        name="pack",
    )(pos, co, h_blocks)


def strings_and_blocks(bits, halves, h_ref, column, pair, take):
    strings, blocks = [], []
    for i in range(8):
        start = pl.multiple_of(bits[pair, i] * W, W)
        strings.append(take(halves[i % 2], i // 2, start))
        blocks.append(h_ref[column, i])
    return strings, jnp.concatenate(blocks, axis=0)


def direct_kernel(where, bits, low, high, h_ref, out_ref, kept_ref):
    for column in range(4):
        strings, blocks = strings_and_blocks(
            bits,
            (low, high),
            h_ref,
            column,
            column * 2 + where[2],
            lambda ref, t, start: ref[t, :, pl.ds(start, W)],
        )
        part = jnp.dot(jnp.concatenate(strings, axis=1), blocks, preferred_element_type=jnp.float32)
        out_ref[column] = part.astype(jnp.bfloat16)

        @pl.when(where[1] == column)
        def _():
            kept_ref[...] = part


def mirror_kernel(where, bits, low, high, own_ref, other_ref, out_ref, kept_ref):
    for column in range(4):
        for h_ref, half in ((own_ref, where[2]), (other_ref, 1 - where[2])):
            strings, blocks = strings_and_blocks(
                bits,
                (low, high),
                h_ref,
                column,
                column * 2 + half,
                lambda ref, t, start: ref[t, pl.ds(start, W), :],
            )
            part = lax.dot_general(
                blocks,
                jnp.concatenate(strings, axis=0),
                (((0,), (0,)), ((), ())),
                preferred_element_type=jnp.float32,
            )
            rows = pl.ds(pl.multiple_of(half * 2 * W, 2 * W), 2 * W)
            out_ref[column, rows, :] = part.astype(jnp.bfloat16)

            @pl.when(where[1] == column)
            def _():
                kept_ref[rows, :] = part


def partial_sums(kernel, name, shape, where, bits, tiles, *hams):
    return pl.pallas_call(
        kernel,
        out_shape=(
            jax.ShapeDtypeStruct((4, *shape), jnp.bfloat16),
            jax.ShapeDtypeStruct(shape, jnp.float32),
        ),
        in_specs=[pl.BlockSpec(memory_space=pltpu.SMEM)] * 2
        + [pl.BlockSpec(memory_space=pltpu.VMEM)] * (2 + len(hams)),
        out_specs=(pl.BlockSpec(memory_space=pltpu.VMEM), pl.BlockSpec(memory_space=pltpu.VMEM)),
        compiler_params=PARAMS,
        name=name,
    )(where, bits, *tiles, *hams)


def exchanged(parts):
    return lax.all_to_all(parts, "x", 0, 0, tiled=True)


def summed(got, kept, x):
    others = (jnp.arange(4) != x)[:, None, None]
    return kept + jnp.sum(jnp.where(others, got, jnp.zeros_like(got)).astype(jnp.float32), axis=0)


def on_device(coeffs, diag_energy, energy, h_blocks, pattern, counts):
    zl, x, zh, y, co = (lax.axis_index(a).astype(jnp.int32) for a in AXES)
    row_id = zl * 4 + x
    slots = h_blocks.shape[1]

    half = coeffs.astype(jnp.bfloat16)

    first, last = half[:256], half[256:]
    here = turned(jnp.where(co == 0, first, last), 0)
    there = turned(jnp.where(co == 0, last, first), 1)
    mirror_halves = [lax.all_gather(part, "zl") for part in (first, last)]
    here, there, *mirror_halves = lax.optimization_barrier((here, there, *mirror_halves))
    tile = (jnp.where(co == 0, here, there), jnp.where(co == 0, there, here))
    direct_halves = [lax.all_gather(part, "zl") for part in tile]

    filled = jnp.arange(slots, dtype=jnp.int32)[None, :] < counts[:, None]
    begin = row_id * 4 + co * 2
    blk = lax.dynamic_slice_in_dim(pattern, begin, 2, 0)
    live = lax.dynamic_slice_in_dim(filled, begin, 2, 0)
    owner = blk // 4
    at = (owner % 4) * 8 + (owner // 4) * 2 + (blk % 4) // 2
    packed = pack(jnp.where(live, at, -1), co[None], h_blocks)
    packed = lax.optimization_barrier((packed, *tile))[0]
    own = lax.all_to_all(packed.reshape(4, 8, W, 2 * W), "x", 0, 0, tiled=True)
    other = swap_cores(lax.optimization_barrier((own, direct_halves[0]))[0])

    names = lax.dynamic_slice_in_dim(pattern, zl * 16, 16, 0).reshape(8, 1, 2 * slots)
    i = jnp.arange(8, dtype=jnp.int32)
    odd = (8 * (i // 2) + 2 * x + i % 2) * 2 + 1
    bits = jnp.any(names == odd[None, :, None], axis=2).astype(jnp.int32)
    here_first = jnp.stack([zl, x, co])
    there_first = jnp.stack([zl, x, 1 - co])

    upper, kept_upper = partial_sums(direct_kernel, "direct", (256, 256), here_first, bits, direct_halves, own)
    got_upper = exchanged(upper)
    direct_halves[1], upper = lax.optimization_barrier((direct_halves[1], upper))
    lower, kept_lower = partial_sums(direct_kernel, "direct", (256, 256), there_first, bits, direct_halves, other)
    lower, got_upper = lax.optimization_barrier((lower, got_upper))
    got_lower = exchanged(lower)
    mirror_halves[1], lower = lax.optimization_barrier((mirror_halves[1], lower))
    mirror, kept = partial_sums(
        mirror_kernel, "mirror", (512, 256), here_first, bits, mirror_halves, own, other
    )
    here = turned(summed(got_upper, kept_upper, x).astype(jnp.bfloat16), 0)
    got_lower, mirror = lax.optimization_barrier((got_lower, mirror))
    there = turned(summed(got_lower, kept_lower, x).astype(jnp.bfloat16), 1)
    mirror_term = summed(exchanged(mirror), kept, x)
    direct_term = jnp.where(
        co == 0, jnp.concatenate([here, there], axis=0), jnp.concatenate([there, here], axis=0)
    ).astype(jnp.float32)

    sigma_full = direct_term + mirror_term + diag_energy * coeffs
    shift_value = energy[0]
    return (sigma_full - shift_value * coeffs) / jnp.maximum(jnp.abs(diag_energy - shift_value), 1.0)


def solution(mesh):
    fine = Mesh(mesh.devices.reshape(4, 4, 4, 4, 2), AXES)
    placed = (P(ROW, COL), P(ROW, COL), P(), P(ROW, None, None, None), P(), P())
    return jax.shard_map(on_device, mesh=fine, in_specs=placed, out_specs=P(ROW, COL), check_vma=False)
```

```python
import jax
import jax.numpy as jnp
from jax import lax
from jax.experimental import pallas as pl
from jax.experimental.pallas import tpu as pltpu
from jax.sharding import Mesh, PartitionSpec as P

AXES = ("zl", "x", "zh", "y", "co")
ROW = ("zl", "x")
COL = ("zh", "y", "co")
W = 128
VMEM_LIMIT = 56 * 1024 * 1024
PARAMS = pltpu.CompilerParams(vmem_limit_bytes=VMEM_LIMIT)


def shifted(value, axis, step):
    return lax.ppermute(value, axis, [(i, (i + step) % 4) for i in range(4)])


def swap_cores(value):
    return lax.ppermute(value, "co", [(0, 1), (1, 0)])


def turned(value, cross):
    pairs = [
        ((r * 16 + k) * 2 + c, (k * 16 + r) * 2 + (c ^ cross))
        for r in range(16)
        for k in range(16)
        for c in range(2)
    ]
    return lax.ppermute(value, AXES, pairs)


def pack_kernel(pos, co, h_ref, out_ref):
    out_ref[...] = jnp.zeros_like(out_ref)
    for m in range(2):

        def place(s, carry, m=m):
            at = pos[m, s]

            @pl.when(at >= 0)
            def _():
                out_ref[at, :, m * W : (m + 1) * W] = h_ref[m, s]

            return carry

        lax.fori_loop(0, h_ref.shape[1], place, 0)


def pack(pos, co, h_blocks):
    slots = h_blocks.shape[1]
    return pl.pallas_call(
        pack_kernel,
        out_shape=jax.ShapeDtypeStruct((32, W, 2 * W), jnp.bfloat16),
        grid_spec=pltpu.PrefetchScalarGridSpec(
            num_scalar_prefetch=2,
            grid=(1,),
            in_specs=[pl.BlockSpec((2, slots, W, W), lambda i, pos, co: (co[0], 0, 0, 0))],
            out_specs=pl.BlockSpec((32, W, 2 * W), lambda i, pos, co: (0, 0, 0)),
        ),
        compiler_params=PARAMS,
        name="pack",
    )(pos, co, h_blocks)


def strings_and_blocks(where, bits, tiles, h_ref, column, pair, take):
    strings, blocks = [], []
    for d, tile in enumerate(tiles):
        owner = lax.rem(where[0] - d + 4, 4)
        for j in range(2):
            i = owner * 2 + j
            start = pl.multiple_of((2 * j + bits[pair, i]) * W, W)
            strings.append(take(tile, start))
            blocks.append(h_ref[column, i])
    return strings, jnp.concatenate(blocks, axis=0)


def direct_kernel(where, bits, t0, t1, t2, t3, h_ref, out_ref, kept_ref):
    for column in range(4):
        strings, blocks = strings_and_blocks(
            where,
            bits,
            (t0, t1, t2, t3),
            h_ref,
            column,
            column * 2 + where[2],
            lambda tile, start: tile[:, pl.ds(start, W)],
        )
        part = jnp.dot(jnp.concatenate(strings, axis=1), blocks, preferred_element_type=jnp.float32)
        out_ref[column] = part.astype(jnp.bfloat16)

        @pl.when(where[1] == column)
        def _():
            kept_ref[...] = part


def mirror_kernel(where, bits, t0, t1, t2, t3, own_ref, other_ref, out_ref, kept_ref):
    for column in range(4):
        for h_ref, half in ((own_ref, where[2]), (other_ref, 1 - where[2])):
            strings, blocks = strings_and_blocks(
                where,
                bits,
                (t0, t1, t2, t3),
                h_ref,
                column,
                column * 2 + half,
                lambda tile, start: tile[pl.ds(start, W), :],
            )
            part = lax.dot_general(
                blocks,
                jnp.concatenate(strings, axis=0),
                (((0,), (0,)), ((), ())),
                preferred_element_type=jnp.float32,
            )
            rows = pl.ds(pl.multiple_of(half * 2 * W, 2 * W), 2 * W)
            out_ref[column, rows, :] = part.astype(jnp.bfloat16)

            @pl.when(where[1] == column)
            def _():
                kept_ref[rows, :] = part


def partial_sums(kernel, name, shape, where, bits, tiles, *hams):
    return pl.pallas_call(
        kernel,
        out_shape=(
            jax.ShapeDtypeStruct((4, *shape), jnp.bfloat16),
            jax.ShapeDtypeStruct(shape, jnp.float32),
        ),
        in_specs=[pl.BlockSpec(memory_space=pltpu.SMEM)] * 2
        + [pl.BlockSpec(memory_space=pltpu.VMEM)] * (4 + len(hams)),
        out_specs=(pl.BlockSpec(memory_space=pltpu.VMEM), pl.BlockSpec(memory_space=pltpu.VMEM)),
        compiler_params=PARAMS,
        cost_estimate=pl.CostEstimate(flops=20_000_000_000, bytes_accessed=40_000_000, transcendentals=0),
        name=name,
    )(where, bits, *tiles, *hams)


def exchanged(parts):
    return lax.all_to_all(parts, "x", 0, 0, tiled=True)


def summed(got, kept, x):
    others = (jnp.arange(4) != x)[:, None, None]
    return kept + jnp.sum(jnp.where(others, got, jnp.zeros_like(got)).astype(jnp.float32), axis=0)


def on_device(coeffs, diag_energy, energy, h_blocks, pattern, counts):
    zl, x, zh, y, co = (lax.axis_index(a).astype(jnp.int32) for a in AXES)
    row_id = zl * 4 + x
    slots = h_blocks.shape[1]

    half = coeffs.astype(jnp.bfloat16)

    first, last = half[:256], half[256:]
    here = turned(jnp.where(co == 0, first, last), 0)
    there = turned(jnp.where(co == 0, last, first), 1)
    tile = jnp.where(
        co == 0, jnp.concatenate([here, there], axis=1), jnp.concatenate([there, here], axis=1)
    )
    mirror_tiles = [half] + [shifted(half, "zl", d) for d in (1, 2, 3)]
    tile = lax.optimization_barrier((tile, *mirror_tiles[1:]))[0]
    direct_tiles = [tile] + [shifted(tile, "zl", d) for d in (1, 2, 3)]

    filled = jnp.arange(slots, dtype=jnp.int32)[None, :] < counts[:, None]
    begin = row_id * 4 + co * 2
    blk = lax.dynamic_slice_in_dim(pattern, begin, 2, 0)
    live = lax.dynamic_slice_in_dim(filled, begin, 2, 0)
    owner = blk // 4
    at = (owner % 4) * 8 + (owner // 4) * 2 + (blk % 4) // 2
    packed = pack(jnp.where(live, at, -1), co[None], h_blocks)
    own = lax.all_to_all(packed.reshape(4, 8, W, 2 * W), "x", 0, 0, tiled=True)
    other = swap_cores(lax.optimization_barrier((own, tile))[0])

    names = lax.dynamic_slice_in_dim(pattern, zl * 16, 16, 0).reshape(8, 1, 2 * slots)
    i = jnp.arange(8, dtype=jnp.int32)
    odd = (8 * (i // 2) + 2 * x + i % 2) * 2 + 1
    bits = jnp.any(names == odd[None, :, None], axis=2).astype(jnp.int32)
    here_first = jnp.stack([zl, x, co])
    there_first = jnp.stack([zl, x, 1 - co])

    mirror, kept = partial_sums(
        mirror_kernel, "mirror", (512, 256), here_first, bits, mirror_tiles, own, other
    )
    got = exchanged(mirror)
    direct_tiles[3], mirror = lax.optimization_barrier((direct_tiles[3], mirror))
    upper, kept_upper = partial_sums(direct_kernel, "direct", (256, 256), here_first, bits, direct_tiles, own)
    upper, got = lax.optimization_barrier((upper, got))
    got_upper = exchanged(upper)
    direct_tiles[3], upper = lax.optimization_barrier((direct_tiles[3], upper))
    lower, kept_lower = partial_sums(direct_kernel, "direct", (256, 256), there_first, bits, direct_tiles, other)
    lower, got_upper = lax.optimization_barrier((lower, got_upper))
    got_lower = exchanged(lower)
    here = turned(summed(got_upper, kept_upper, x).astype(jnp.bfloat16), 0)
    there = turned(summed(got_lower, kept_lower, x).astype(jnp.bfloat16), 1)
    mirror_term = summed(got, kept, x)
    direct_term = jnp.where(
        co == 0, jnp.concatenate([here, there], axis=0), jnp.concatenate([there, here], axis=0)
    ).astype(jnp.float32)

    sigma_full = direct_term + mirror_term + diag_energy * coeffs
    shift_value = energy[0]
    return (sigma_full - shift_value * coeffs) / jnp.maximum(jnp.abs(diag_energy - shift_value), 1.0)


def solution(mesh):
    fine = Mesh(mesh.devices.reshape(4, 4, 4, 4, 2), AXES)
    placed = (P(ROW, COL), P(ROW, COL), P(), P(ROW, None, None, None), P(), P())
    return jax.shard_map(on_device, mesh=fine, in_specs=placed, out_specs=P(ROW, COL), check_vma=False)
```

```python
import jax
import jax.numpy as jnp
from jax import lax
from jax.experimental import pallas as pl
from jax.experimental.pallas import tpu as pltpu
from jax.sharding import Mesh, PartitionSpec as P

AXES = ("zl", "x", "zh", "y", "co")
ROW = ("zl", "x")
COL = ("zh", "y", "co")
W = 128
VMEM_LIMIT = 56 * 1024 * 1024
PARAMS = pltpu.CompilerParams(vmem_limit_bytes=VMEM_LIMIT)


def shifted(value, axis, step):
    return lax.ppermute(value, axis, [(i, (i + step) % 4) for i in range(4)])


def swap_cores(value):
    return lax.ppermute(value, "co", [(0, 1), (1, 0)])


def turned(value, cross):
    pairs = [
        ((r * 16 + k) * 2 + c, (k * 16 + r) * 2 + (c ^ cross))
        for r in range(16)
        for k in range(16)
        for c in range(2)
    ]
    return lax.ppermute(value, AXES, pairs)


def pack_kernel(pos, co, h_ref, out_ref):
    out_ref[...] = jnp.zeros_like(out_ref)
    for m in range(2):

        def place(s, carry, m=m):
            at = pos[m, s]

            @pl.when(at >= 0)
            def _():
                out_ref[at, :, m * W : (m + 1) * W] = h_ref[m, s]

            return carry

        lax.fori_loop(0, h_ref.shape[1], place, 0)


def pack(pos, co, h_blocks):
    slots = h_blocks.shape[1]
    return pl.pallas_call(
        pack_kernel,
        out_shape=jax.ShapeDtypeStruct((32, W, 2 * W), jnp.bfloat16),
        grid_spec=pltpu.PrefetchScalarGridSpec(
            num_scalar_prefetch=2,
            grid=(1,),
            in_specs=[pl.BlockSpec((2, slots, W, W), lambda i, pos, co: (co[0], 0, 0, 0))],
            out_specs=pl.BlockSpec((32, W, 2 * W), lambda i, pos, co: (0, 0, 0)),
        ),
        compiler_params=PARAMS,
        name="pack",
    )(pos, co, h_blocks)


def strings_and_blocks(where, bits, tiles, h_ref, column, pair, take):
    strings, blocks = [], []
    for d, tile in enumerate(tiles):
        owner = lax.rem(where[0] - d + 4, 4)
        for j in range(2):
            i = owner * 2 + j
            start = pl.multiple_of((2 * j + bits[pair, i]) * W, W)
            strings.append(take(tile, start))
            blocks.append(h_ref[column, i])
    return strings, jnp.concatenate(blocks, axis=0)


def direct_kernel(where, bits, t0, t1, t2, t3, h_ref, out_ref, kept_ref):
    for column in range(4):
        strings, blocks = strings_and_blocks(
            where,
            bits,
            (t0, t1, t2, t3),
            h_ref,
            column,
            column * 2 + where[2],
            lambda tile, start: tile[:, pl.ds(start, W)],
        )
        part = jnp.dot(jnp.concatenate(strings, axis=1), blocks, preferred_element_type=jnp.float32)
        out_ref[column] = part.astype(jnp.bfloat16)

        @pl.when(where[1] == column)
        def _():
            kept_ref[...] = part


def mirror_kernel(where, bits, t0, t1, t2, t3, own_ref, other_ref, out_ref, kept_ref):
    for column in range(4):
        for h_ref, half in ((own_ref, where[2]), (other_ref, 1 - where[2])):
            strings, blocks = strings_and_blocks(
                where,
                bits,
                (t0, t1, t2, t3),
                h_ref,
                column,
                column * 2 + half,
                lambda tile, start: tile[pl.ds(start, W), :],
            )
            part = lax.dot_general(
                blocks,
                jnp.concatenate(strings, axis=0),
                (((0,), (0,)), ((), ())),
                preferred_element_type=jnp.float32,
            )
            rows = pl.ds(pl.multiple_of(half * 2 * W, 2 * W), 2 * W)
            out_ref[column, rows, :] = part.astype(jnp.bfloat16)

            @pl.when(where[1] == column)
            def _():
                kept_ref[rows, :] = part


def partial_sums(kernel, name, shape, where, bits, tiles, *hams):
    return pl.pallas_call(
        kernel,
        out_shape=(
            jax.ShapeDtypeStruct((4, *shape), jnp.bfloat16),
            jax.ShapeDtypeStruct(shape, jnp.float32),
        ),
        in_specs=[pl.BlockSpec(memory_space=pltpu.SMEM)] * 2
        + [pl.BlockSpec(memory_space=pltpu.VMEM)] * (4 + len(hams)),
        out_specs=(pl.BlockSpec(memory_space=pltpu.VMEM), pl.BlockSpec(memory_space=pltpu.VMEM)),
        compiler_params=PARAMS,
        cost_estimate=pl.CostEstimate(flops=20_000_000_000, bytes_accessed=40_000_000, transcendentals=0),
        name=name,
    )(where, bits, *tiles, *hams)


def base_kernel(co, energy, here_ref, there_ref, coeffs_ref, diag_ref, out_ref):
    for at, ref in ((co[0], here_ref), (1 - co[0], there_ref)):
        rows = pl.ds(pl.multiple_of(at * 256, 256), 256)
        coeffs = coeffs_ref[rows, :]
        out_ref[rows, :] = ref[...].astype(jnp.float32) + diag_ref[rows, :] * coeffs - energy[0] * coeffs


def direct_base(co, energy, here, there, coeffs, diag_energy):
    return pl.pallas_call(
        base_kernel,
        out_shape=jax.ShapeDtypeStruct(coeffs.shape, jnp.float32),
        in_specs=[pl.BlockSpec(memory_space=pltpu.SMEM)] * 2 + [pl.BlockSpec(memory_space=pltpu.VMEM)] * 4,
        out_specs=pl.BlockSpec(memory_space=pltpu.VMEM),
        compiler_params=PARAMS,
        cost_estimate=pl.CostEstimate(flops=20_000_000_000, bytes_accessed=40_000_000, transcendentals=0),
        name="base",
    )(co, energy, here, there, coeffs, diag_energy)


def exchanged(parts):
    return lax.all_to_all(parts, "x", 0, 0, tiled=True)


def summed(got, kept, x):
    others = (jnp.arange(4) != x)[:, None, None]
    return kept + jnp.sum(jnp.where(others, got, jnp.zeros_like(got)).astype(jnp.float32), axis=0)


def on_device(coeffs, diag_energy, energy, h_blocks, pattern, counts):
    zl, x, zh, y, co = (lax.axis_index(a).astype(jnp.int32) for a in AXES)
    row_id = zl * 4 + x
    slots = h_blocks.shape[1]

    half = coeffs.astype(jnp.bfloat16)

    first, last = half[:256], half[256:]
    here = turned(jnp.where(co == 0, first, last), 0)
    there = turned(jnp.where(co == 0, last, first), 1)
    tile = jnp.where(
        co == 0, jnp.concatenate([here, there], axis=1), jnp.concatenate([there, here], axis=1)
    )
    direct_tiles = [tile] + [shifted(tile, "zl", d) for d in (1, 2, 3)]
    later = lax.optimization_barrier((half, *direct_tiles[1:]))[0]
    mirror_tiles = [half] + [shifted(later, "zl", d) for d in (1, 2, 3)]

    filled = jnp.arange(slots, dtype=jnp.int32)[None, :] < counts[:, None]
    begin = row_id * 4 + co * 2
    blk = lax.dynamic_slice_in_dim(pattern, begin, 2, 0)
    live = lax.dynamic_slice_in_dim(filled, begin, 2, 0)
    owner = blk // 4
    at = (owner % 4) * 8 + (owner // 4) * 2 + (blk % 4) // 2
    packed = pack(jnp.where(live, at, -1), co[None], h_blocks)
    packed = lax.optimization_barrier((packed, tile))[0]
    own = lax.all_to_all(packed.reshape(4, 8, W, 2 * W), "x", 0, 0, tiled=True)
    other = swap_cores(lax.optimization_barrier((own, *direct_tiles[1:]))[0])

    names = lax.dynamic_slice_in_dim(pattern, zl * 16, 16, 0).reshape(8, 1, 2 * slots)
    i = jnp.arange(8, dtype=jnp.int32)
    odd = (8 * (i // 2) + 2 * x + i % 2) * 2 + 1
    bits = jnp.any(names == odd[None, :, None], axis=2).astype(jnp.int32)
    here_first = jnp.stack([zl, x, co])
    there_first = jnp.stack([zl, x, 1 - co])

    upper, kept_upper = partial_sums(direct_kernel, "direct", (256, 256), here_first, bits, direct_tiles, own)
    got_upper = exchanged(upper)
    direct_tiles[3], upper = lax.optimization_barrier((direct_tiles[3], upper))
    lower, kept_lower = partial_sums(direct_kernel, "direct", (256, 256), there_first, bits, direct_tiles, other)
    lower, got_upper, mirror_tiles[1], mirror_tiles[3] = lax.optimization_barrier(
        (lower, got_upper, mirror_tiles[1], mirror_tiles[3])
    )
    got_lower = exchanged(lower)
    upper = summed(got_upper, kept_upper, x).astype(jnp.bfloat16)
    lower = summed(got_lower, kept_lower, x).astype(jnp.bfloat16)
    here, there = turned(upper, 0), turned(lower, 1)
    mirror_tiles[3], lower = lax.optimization_barrier((mirror_tiles[3], lower))
    mirror, kept = partial_sums(
        mirror_kernel, "mirror", (512, 256), here_first, bits, mirror_tiles, own, other
    )
    mirror_term = summed(exchanged(mirror), kept, x)
    base = direct_base(co[None], energy, here, there, coeffs, diag_energy)
    return (base + mirror_term) / jnp.maximum(jnp.abs(diag_energy - energy[0]), 1.0)


def solution(mesh):
    fine = Mesh(mesh.devices.reshape(4, 4, 4, 4, 2), AXES)
    placed = (P(ROW, COL), P(ROW, COL), P(), P(ROW, None, None, None), P(), P())
    return jax.shard_map(on_device, mesh=fine, in_specs=placed, out_specs=P(ROW, COL), check_vma=False)
```

```python
import jax
import jax.numpy as jnp
from jax import lax
from jax.experimental import pallas as pl
from jax.experimental.pallas import tpu as pltpu
from jax.sharding import Mesh, PartitionSpec as P

AXES = ("zl", "x", "zh", "y", "co")
ROW = ("zl", "x")
COL = ("zh", "y", "co")
W = 128
STEP = 24_000_000_000
LATE = 2_000_000_000
VMEM_LIMIT = 56 * 1024 * 1024
PARAMS = pltpu.CompilerParams(vmem_limit_bytes=VMEM_LIMIT)


def shifted(value, axis, step):
    return lax.ppermute(value, axis, [(i, (i + step) % 4) for i in range(4)])


def swap_cores(value):
    return lax.ppermute(value, "co", [(0, 1), (1, 0)])


def turned(value, cross):
    pairs = [
        ((r * 16 + k) * 2 + c, (k * 16 + r) * 2 + (c ^ cross))
        for r in range(16)
        for k in range(16)
        for c in range(2)
    ]
    return lax.ppermute(value, AXES, pairs)


def pack_kernel(pos, co, h_ref, out_ref):
    out_ref[...] = jnp.zeros_like(out_ref)
    for m in range(2):

        def place(s, carry, m=m):
            at = pos[m, s]

            @pl.when(at >= 0)
            def _():
                out_ref[at, :, m * W : (m + 1) * W] = h_ref[m, s]

            return carry

        lax.fori_loop(0, h_ref.shape[1], place, 0)


def pack(pos, co, h_blocks):
    slots = h_blocks.shape[1]
    return pl.pallas_call(
        pack_kernel,
        out_shape=jax.ShapeDtypeStruct((32, W, 2 * W), jnp.bfloat16),
        grid_spec=pltpu.PrefetchScalarGridSpec(
            num_scalar_prefetch=2,
            grid=(1,),
            in_specs=[pl.BlockSpec((2, slots, W, W), lambda i, pos, co: (co[0], 0, 0, 0))],
            out_specs=pl.BlockSpec((32, W, 2 * W), lambda i, pos, co: (0, 0, 0)),
        ),
        compiler_params=PARAMS,
        name="pack",
    )(pos, co, h_blocks)


def strings_and_blocks(where, bits, tiles, h_ref, column, pair, take):
    strings, blocks = [], []
    for d, tile in enumerate(tiles):
        owner = lax.rem(where[0] - d + 4, 4)
        for j in range(2):
            i = owner * 2 + j
            start = pl.multiple_of((2 * j + bits[pair, i]) * W, W)
            strings.append(take(tile, start))
            blocks.append(h_ref[column, i])
    return strings, jnp.concatenate(blocks, axis=0)


def direct_kernel(where, bits, t0, t1, t2, t3, h_ref, out_ref, kept_ref):
    for column in range(4):
        strings, blocks = strings_and_blocks(
            where,
            bits,
            (t0, t1, t2, t3),
            h_ref,
            column,
            column * 2 + where[2],
            lambda tile, start: tile[:, pl.ds(start, W)],
        )
        part = jnp.dot(jnp.concatenate(strings, axis=1), blocks, preferred_element_type=jnp.float32)
        out_ref[column] = part.astype(jnp.bfloat16)

        @pl.when(where[1] == column)
        def _():
            kept_ref[...] = part


def mirror_kernel(where, bits, t0, t1, t2, t3, own_ref, other_ref, out_ref, kept_ref):
    for column in range(4):
        for h_ref, half in ((own_ref, where[2]), (other_ref, 1 - where[2])):
            strings, blocks = strings_and_blocks(
                where,
                bits,
                (t0, t1, t2, t3),
                h_ref,
                column,
                column * 2 + half,
                lambda tile, start: tile[pl.ds(start, W), :],
            )
            part = lax.dot_general(
                blocks,
                jnp.concatenate(strings, axis=0),
                (((0,), (0,)), ((), ())),
                preferred_element_type=jnp.float32,
            )
            rows = pl.ds(pl.multiple_of(half * 2 * W, 2 * W), 2 * W)
            out_ref[column, rows, :] = part.astype(jnp.bfloat16)

            @pl.when(where[1] == column)
            def _():
                kept_ref[rows, :] = part


def partial_sums(kernel, name, shape, where, bits, tiles, *hams):
    return pl.pallas_call(
        kernel,
        out_shape=(
            jax.ShapeDtypeStruct((4, *shape), jnp.bfloat16),
            jax.ShapeDtypeStruct(shape, jnp.float32),
        ),
        in_specs=[pl.BlockSpec(memory_space=pltpu.SMEM)] * 2
        + [pl.BlockSpec(memory_space=pltpu.VMEM)] * (4 + len(hams)),
        out_specs=(pl.BlockSpec(memory_space=pltpu.VMEM), pl.BlockSpec(memory_space=pltpu.VMEM)),
        compiler_params=PARAMS,
        cost_estimate=pl.CostEstimate(flops=20_000_000_000, bytes_accessed=40_000_000, transcendentals=0),
        name=name,
    )(where, bits, *tiles, *hams)


def base_kernel(co, energy, here_ref, there_ref, coeffs_ref, diag_ref, out_ref):
    for at, ref in ((co[0], here_ref), (1 - co[0], there_ref)):
        rows = pl.ds(pl.multiple_of(at * 256, 256), 256)
        coeffs = coeffs_ref[rows, :]
        out_ref[rows, :] = ref[...].astype(jnp.float32) + diag_ref[rows, :] * coeffs - energy[0] * coeffs


def direct_base(co, energy, here, there, coeffs, diag_energy):
    return pl.pallas_call(
        base_kernel,
        out_shape=jax.ShapeDtypeStruct(coeffs.shape, jnp.float32),
        in_specs=[pl.BlockSpec(memory_space=pltpu.SMEM)] * 2 + [pl.BlockSpec(memory_space=pltpu.VMEM)] * 4,
        out_specs=pl.BlockSpec(memory_space=pltpu.VMEM),
        compiler_params=PARAMS,
        cost_estimate=pl.CostEstimate(flops=20_000_000_000, bytes_accessed=40_000_000, transcendentals=0),
        name="base",
    )(co, energy, here, there, coeffs, diag_energy)


def copy_kernel(in_ref, out_ref):
    out_ref[...] = in_ref[...]


def step_kernel(value, flops):
    return pl.pallas_call(
        copy_kernel,
        out_shape=jax.ShapeDtypeStruct(value.shape, value.dtype),
        in_specs=[pl.BlockSpec(memory_space=pltpu.VMEM)],
        out_specs=pl.BlockSpec(memory_space=pltpu.VMEM),
        cost_estimate=pl.CostEstimate(flops=flops, bytes_accessed=1000, transcendentals=0),
        name="step",
    )(value)


def exchanged(parts):
    return lax.all_to_all(parts, "x", 0, 0, tiled=True)


def summed(got, kept, x):
    others = (jnp.arange(4) != x)[:, None, None]
    return kept + jnp.sum(jnp.where(others, got, jnp.zeros_like(got)).astype(jnp.float32), axis=0)


def on_device(coeffs, diag_energy, energy, h_blocks, pattern, counts):
    zl, x, zh, y, co = (lax.axis_index(a).astype(jnp.int32) for a in AXES)
    row_id = zl * 4 + x
    slots = h_blocks.shape[1]

    half = coeffs.astype(jnp.bfloat16)

    first, last = half[:256], half[256:]
    here = turned(jnp.where(co == 0, first, last), 0)
    there = turned(jnp.where(co == 0, last, first), 1)
    tile = jnp.where(
        co == 0, jnp.concatenate([here, there], axis=1), jnp.concatenate([there, here], axis=1)
    )
    filled = jnp.arange(slots, dtype=jnp.int32)[None, :] < counts[:, None]
    begin = row_id * 4 + co * 2
    blk = lax.dynamic_slice_in_dim(pattern, begin, 2, 0)
    live = lax.dynamic_slice_in_dim(filled, begin, 2, 0)
    owner = blk // 4
    at = (owner % 4) * 8 + (owner // 4) * 2 + (blk % 4) // 2
    packed = pack(jnp.where(live, at, -1), co[None], h_blocks)
    packed, tile = lax.optimization_barrier((packed, tile))
    direct_tiles = [tile] + [shifted(tile, "zl", d) for d in (1, 2, 3)]
    later = lax.optimization_barrier((half, *direct_tiles[1:]))[0]
    mirror_tiles = [half] + [shifted(later, "zl", d) for d in (1, 2, 3)]
    own = lax.all_to_all(packed.reshape(4, 8, W, 2 * W), "x", 0, 0, tiled=True)
    names = lax.dynamic_slice_in_dim(pattern, zl * 16, 16, 0).reshape(8, 1, 2 * slots)
    i = jnp.arange(8, dtype=jnp.int32)
    odd = (8 * (i // 2) + 2 * x + i % 2) * 2 + 1
    bits = jnp.any(names == odd[None, :, None], axis=2).astype(jnp.int32)
    bits = step_kernel(lax.optimization_barrier((bits, *direct_tiles[1:]))[0], STEP)
    other = swap_cores(lax.optimization_barrier((own, bits))[0])
    here_first = jnp.stack([zl, x, co])
    there_first = jnp.stack([zl, x, 1 - co])

    upper, kept_upper = partial_sums(direct_kernel, "direct", (256, 256), here_first, bits, direct_tiles, own)
    got_upper = exchanged(upper)
    direct_tiles[3], upper = lax.optimization_barrier((direct_tiles[3], upper))
    lower, kept_lower = partial_sums(direct_kernel, "direct", (256, 256), there_first, bits, direct_tiles, other)
    lower, got_upper = lax.optimization_barrier((lower, got_upper))
    got_lower = exchanged(lower)
    upper = summed(got_upper, kept_upper, x).astype(jnp.bfloat16)
    bits, _, *mirror_tiles = lax.optimization_barrier((bits, lower, *mirror_tiles))
    bits = step_kernel(bits, LATE)
    got_lower, upper, bits = lax.optimization_barrier((got_lower, upper, bits))
    lower = summed(got_lower, kept_lower, x).astype(jnp.bfloat16)
    here, there = turned(upper, 0), turned(lower, 1)
    mirror, kept = partial_sums(
        mirror_kernel, "mirror", (512, 256), here_first, bits, mirror_tiles, own, other
    )
    mirror_term = summed(exchanged(mirror), kept, x)
    base = direct_base(co[None], energy, here, there, coeffs, diag_energy)
    return (base + mirror_term) / jnp.maximum(jnp.abs(diag_energy - energy[0]), 1.0)


def solution(mesh):
    fine = Mesh(mesh.devices.reshape(4, 4, 4, 4, 2), AXES)
    placed = (P(ROW, COL), P(ROW, COL), P(), P(ROW, None, None, None), P(), P())
    return jax.shard_map(on_device, mesh=fine, in_specs=placed, out_specs=P(ROW, COL), check_vma=False)
```

```python
import jax
import jax.numpy as jnp
from jax import lax
from jax.experimental import pallas as pl
from jax.experimental.pallas import tpu as pltpu
from jax.sharding import Mesh, PartitionSpec as P

AXES = ("zl", "x", "zh", "y", "co")
ROW = ("zl", "x")
COL = ("zh", "y", "co")
W = 128
STEP = 16_000_000_000
LATE = 2_000_000_000
VMEM_LIMIT = 56 * 1024 * 1024
PARAMS = pltpu.CompilerParams(vmem_limit_bytes=VMEM_LIMIT)


def shifted(value, axis, step):
    return lax.ppermute(value, axis, [(i, (i + step) % 4) for i in range(4)])


def swap_cores(value):
    return lax.ppermute(value, "co", [(0, 1), (1, 0)])


def turned(value, cross):
    pairs = [
        ((r * 16 + k) * 2 + c, (k * 16 + r) * 2 + (c ^ cross))
        for r in range(16)
        for k in range(16)
        for c in range(2)
    ]
    return lax.ppermute(value, AXES, pairs)


def pack_kernel(pos, co, h_ref, out_ref):
    out_ref[...] = jnp.zeros_like(out_ref)
    for m in range(2):

        def place(s, carry, m=m):
            at = pos[m, s]

            @pl.when(at >= 0)
            def _():
                out_ref[at, :, m * W : (m + 1) * W] = h_ref[m, s]

            return carry

        lax.fori_loop(0, h_ref.shape[1], place, 0)


def pack(pos, co, h_blocks):
    slots = h_blocks.shape[1]
    return pl.pallas_call(
        pack_kernel,
        out_shape=jax.ShapeDtypeStruct((32, W, 2 * W), jnp.bfloat16),
        grid_spec=pltpu.PrefetchScalarGridSpec(
            num_scalar_prefetch=2,
            grid=(1,),
            in_specs=[pl.BlockSpec((2, slots, W, W), lambda i, pos, co: (co[0], 0, 0, 0))],
            out_specs=pl.BlockSpec((32, W, 2 * W), lambda i, pos, co: (0, 0, 0)),
        ),
        compiler_params=PARAMS,
        name="pack",
    )(pos, co, h_blocks)


def strings_and_blocks(where, bits, tiles, h_ref, column, pair, take):
    strings, blocks = [], []
    for d, tile in enumerate(tiles):
        owner = lax.rem(where[0] - d + 4, 4)
        for j in range(2):
            i = owner * 2 + j
            start = pl.multiple_of((2 * j + bits[pair, i]) * W, W)
            strings.append(take(tile, start))
            blocks.append(h_ref[column, i])
    return strings, jnp.concatenate(blocks, axis=0)


def direct_kernel(where, bits, t0, t1, t2, t3, h_ref, out_ref, kept_ref):
    for column in range(4):
        strings, blocks = strings_and_blocks(
            where,
            bits,
            (t0, t1, t2, t3),
            h_ref,
            column,
            column * 2 + where[2],
            lambda tile, start: tile[:, pl.ds(start, W)],
        )
        part = jnp.dot(jnp.concatenate(strings, axis=1), blocks, preferred_element_type=jnp.float32)
        out_ref[column] = part.astype(jnp.bfloat16)

        @pl.when(where[1] == column)
        def _():
            kept_ref[...] = part


def mirror_kernel(where, bits, t0, t1, t2, t3, own_ref, other_ref, out_ref, kept_ref):
    for column in range(4):
        for h_ref, half in ((own_ref, where[2]), (other_ref, 1 - where[2])):
            strings, blocks = strings_and_blocks(
                where,
                bits,
                (t0, t1, t2, t3),
                h_ref,
                column,
                column * 2 + half,
                lambda tile, start: tile[pl.ds(start, W), :],
            )
            part = lax.dot_general(
                blocks,
                jnp.concatenate(strings, axis=0),
                (((0,), (0,)), ((), ())),
                preferred_element_type=jnp.float32,
            )
            rows = pl.ds(pl.multiple_of(half * 2 * W, 2 * W), 2 * W)
            out_ref[column, rows, :] = part.astype(jnp.bfloat16)

            @pl.when(where[1] == column)
            def _():
                kept_ref[rows, :] = part


def partial_sums(kernel, name, shape, where, bits, tiles, *hams):
    return pl.pallas_call(
        kernel,
        out_shape=(
            jax.ShapeDtypeStruct((4, *shape), jnp.bfloat16),
            jax.ShapeDtypeStruct(shape, jnp.float32),
        ),
        in_specs=[pl.BlockSpec(memory_space=pltpu.SMEM)] * 2
        + [pl.BlockSpec(memory_space=pltpu.VMEM)] * (4 + len(hams)),
        out_specs=(pl.BlockSpec(memory_space=pltpu.VMEM), pl.BlockSpec(memory_space=pltpu.VMEM)),
        compiler_params=PARAMS,
        cost_estimate=pl.CostEstimate(flops=20_000_000_000, bytes_accessed=40_000_000, transcendentals=0),
        name=name,
    )(where, bits, *tiles, *hams)


def base_kernel(co, energy, here_ref, there_ref, coeffs_ref, diag_ref, out_ref):
    for at, ref in ((co[0], here_ref), (1 - co[0], there_ref)):
        rows = pl.ds(pl.multiple_of(at * 256, 256), 256)
        coeffs = coeffs_ref[rows, :]
        out_ref[rows, :] = ref[...].astype(jnp.float32) + diag_ref[rows, :] * coeffs - energy[0] * coeffs


def direct_base(co, energy, here, there, coeffs, diag_energy):
    return pl.pallas_call(
        base_kernel,
        out_shape=jax.ShapeDtypeStruct(coeffs.shape, jnp.float32),
        in_specs=[pl.BlockSpec(memory_space=pltpu.SMEM)] * 2 + [pl.BlockSpec(memory_space=pltpu.VMEM)] * 4,
        out_specs=pl.BlockSpec(memory_space=pltpu.VMEM),
        compiler_params=PARAMS,
        cost_estimate=pl.CostEstimate(flops=20_000_000_000, bytes_accessed=40_000_000, transcendentals=0),
        name="base",
    )(co, energy, here, there, coeffs, diag_energy)


def copy_kernel(in_ref, out_ref):
    out_ref[...] = in_ref[...]


def step_kernel(value, flops):
    return pl.pallas_call(
        copy_kernel,
        out_shape=jax.ShapeDtypeStruct(value.shape, value.dtype),
        in_specs=[pl.BlockSpec(memory_space=pltpu.VMEM)],
        out_specs=pl.BlockSpec(memory_space=pltpu.VMEM),
        cost_estimate=pl.CostEstimate(flops=flops, bytes_accessed=1000, transcendentals=0),
        name="step",
    )(value)


def exchanged(parts):
    return lax.all_to_all(parts, "x", 0, 0, tiled=True)


def summed(got, kept, x):
    others = (jnp.arange(4) != x)[:, None, None]
    return kept + jnp.sum(jnp.where(others, got, jnp.zeros_like(got)).astype(jnp.float32), axis=0)


def on_device(coeffs, diag_energy, energy, h_blocks, pattern, counts):
    zl, x, zh, y, co = (lax.axis_index(a).astype(jnp.int32) for a in AXES)
    row_id = zl * 4 + x
    slots = h_blocks.shape[1]

    half = coeffs.astype(jnp.bfloat16)

    first, last = half[:256], half[256:]
    here = turned(jnp.where(co == 0, first, last), 0)
    there = turned(jnp.where(co == 0, last, first), 1)
    tile = jnp.where(
        co == 0, jnp.concatenate([here, there], axis=1), jnp.concatenate([there, here], axis=1)
    )
    filled = jnp.arange(slots, dtype=jnp.int32)[None, :] < counts[:, None]
    begin = row_id * 4 + co * 2
    blk = lax.dynamic_slice_in_dim(pattern, begin, 2, 0)
    live = lax.dynamic_slice_in_dim(filled, begin, 2, 0)
    owner = blk // 4
    at = (owner % 4) * 8 + (owner // 4) * 2 + (blk % 4) // 2
    packed = pack(jnp.where(live, at, -1), co[None], h_blocks)
    direct_tiles = [tile] + [shifted(tile, "zl", d) for d in (1, 2, 3)]
    later = lax.optimization_barrier((half, *direct_tiles[1:]))[0]
    mirror_tiles = [half] + [shifted(later, "zl", d) for d in (1, 2, 3)]
    own = lax.all_to_all(packed.reshape(4, 8, W, 2 * W), "x", 0, 0, tiled=True)
    names = lax.dynamic_slice_in_dim(pattern, zl * 16, 16, 0).reshape(8, 1, 2 * slots)
    i = jnp.arange(8, dtype=jnp.int32)
    odd = (8 * (i // 2) + 2 * x + i % 2) * 2 + 1
    bits = jnp.any(names == odd[None, :, None], axis=2).astype(jnp.int32)
    bits = step_kernel(lax.optimization_barrier((bits, *direct_tiles[1:]))[0], STEP)
    other = swap_cores(lax.optimization_barrier((own, bits))[0])
    here_first = jnp.stack([zl, x, co])
    there_first = jnp.stack([zl, x, 1 - co])

    upper, kept_upper = partial_sums(direct_kernel, "direct", (256, 256), here_first, bits, direct_tiles, own)
    got_upper = exchanged(upper)
    direct_tiles[3], upper = lax.optimization_barrier((direct_tiles[3], upper))
    lower, kept_lower = partial_sums(direct_kernel, "direct", (256, 256), there_first, bits, direct_tiles, other)
    lower, got_upper = lax.optimization_barrier((lower, got_upper))
    got_lower = exchanged(lower)
    upper = summed(got_upper, kept_upper, x).astype(jnp.bfloat16)
    bits, _, *mirror_tiles = lax.optimization_barrier((bits, lower, *mirror_tiles))
    bits = step_kernel(bits, LATE)
    mirror, kept = partial_sums(
        mirror_kernel, "mirror", (512, 256), here_first, bits, mirror_tiles, own, other
    )
    got_lower, upper, mirror = lax.optimization_barrier((got_lower, upper, mirror))
    lower = summed(got_lower, kept_lower, x).astype(jnp.bfloat16)
    here, there = turned(upper, 0), turned(lower, 1)
    mirror_term = summed(exchanged(mirror), kept, x)
    base = direct_base(co[None], energy, here, there, coeffs, diag_energy)
    return (base + mirror_term) / jnp.maximum(jnp.abs(diag_energy - energy[0]), 1.0)


def solution(mesh):
    fine = Mesh(mesh.devices.reshape(4, 4, 4, 4, 2), AXES)
    placed = (P(ROW, COL), P(ROW, COL), P(), P(ROW, None, None, None), P(), P())
    return jax.shard_map(on_device, mesh=fine, in_specs=placed, out_specs=P(ROW, COL), check_vma=False)
```

```python
import jax
import jax.numpy as jnp
from jax import lax
from jax.experimental import pallas as pl
from jax.experimental.pallas import tpu as pltpu
from jax.sharding import Mesh, PartitionSpec as P

AXES = ("zl", "x", "zh", "y", "co")
ROW = ("zl", "x")
COL = ("zh", "y", "co")
W = 128
STEP = 16_000_000_000
LATE = 2_000_000_000
VMEM_LIMIT = 56 * 1024 * 1024
PARAMS = pltpu.CompilerParams(vmem_limit_bytes=VMEM_LIMIT)


def shifted(value, axis, step):
    return lax.ppermute(value, axis, [(i, (i + step) % 4) for i in range(4)])


def swap_cores(value):
    return lax.ppermute(value, "co", [(0, 1), (1, 0)])


def turned(value, cross):
    pairs = [
        ((r * 16 + k) * 2 + c, (k * 16 + r) * 2 + (c ^ cross))
        for r in range(16)
        for k in range(16)
        for c in range(2)
    ]
    return lax.ppermute(value, AXES, pairs)


def pack_kernel(pos, co, h_ref, out_ref):
    out_ref[...] = jnp.zeros_like(out_ref)
    for m in range(2):

        def place(s, carry, m=m):
            at = pos[m, s]

            @pl.when(at >= 0)
            def _():
                out_ref[at, :, m * W : (m + 1) * W] = h_ref[m, s]

            return carry

        lax.fori_loop(0, h_ref.shape[1], place, 0)


def pack(pos, co, h_blocks):
    slots = h_blocks.shape[1]
    return pl.pallas_call(
        pack_kernel,
        out_shape=jax.ShapeDtypeStruct((32, W, 2 * W), jnp.bfloat16),
        grid_spec=pltpu.PrefetchScalarGridSpec(
            num_scalar_prefetch=2,
            grid=(1,),
            in_specs=[pl.BlockSpec((2, slots, W, W), lambda i, pos, co: (co[0], 0, 0, 0))],
            out_specs=pl.BlockSpec((32, W, 2 * W), lambda i, pos, co: (0, 0, 0)),
        ),
        compiler_params=PARAMS,
        name="pack",
    )(pos, co, h_blocks)


def strings_and_blocks(where, bits, tiles, h_ref, column, pair, take):
    strings, blocks = [], []
    for d, tile in enumerate(tiles):
        owner = lax.rem(where[0] - d + 4, 4)
        for j in range(2):
            i = owner * 2 + j
            start = pl.multiple_of((2 * j + bits[pair, i]) * W, W)
            strings.append(take(tile, start))
            blocks.append(h_ref[column, i])
    return strings, jnp.concatenate(blocks, axis=0)


def direct_kernel(where, bits, t0, t1, t2, t3, own_ref, other_ref, out_ref, kept_ref):
    for column in range(4):
        for order, h_ref in enumerate((own_ref, other_ref)):
            strings, blocks = strings_and_blocks(
                where,
                bits,
                (t0, t1, t2, t3),
                h_ref,
                column,
                column * 2 + (where[2] if order == 0 else 1 - where[2]),
                lambda tile, start: tile[:, pl.ds(start, W)],
            )
            part = jnp.dot(jnp.concatenate(strings, axis=1), blocks, preferred_element_type=jnp.float32)
            rows = slice(order * 256, (order + 1) * 256)
            out_ref[column, rows, :] = part.astype(jnp.bfloat16)

            @pl.when(where[1] == column)
            def _():
                kept_ref[rows, :] = part


def mirror_kernel(where, bits, t0, t1, t2, t3, own_ref, other_ref, out_ref, kept_ref):
    for column in range(4):
        for h_ref, half in ((own_ref, where[2]), (other_ref, 1 - where[2])):
            strings, blocks = strings_and_blocks(
                where,
                bits,
                (t0, t1, t2, t3),
                h_ref,
                column,
                column * 2 + half,
                lambda tile, start: tile[pl.ds(start, W), :],
            )
            part = lax.dot_general(
                blocks,
                jnp.concatenate(strings, axis=0),
                (((0,), (0,)), ((), ())),
                preferred_element_type=jnp.float32,
            )
            rows = pl.ds(pl.multiple_of(half * 2 * W, 2 * W), 2 * W)
            out_ref[column, rows, :] = part.astype(jnp.bfloat16)

            @pl.when(where[1] == column)
            def _():
                kept_ref[rows, :] = part


def partial_sums(kernel, name, shape, where, bits, tiles, *hams):
    return pl.pallas_call(
        kernel,
        out_shape=(
            jax.ShapeDtypeStruct((4, *shape), jnp.bfloat16),
            jax.ShapeDtypeStruct(shape, jnp.float32),
        ),
        in_specs=[pl.BlockSpec(memory_space=pltpu.SMEM)] * 2
        + [pl.BlockSpec(memory_space=pltpu.VMEM)] * (4 + len(hams)),
        out_specs=(pl.BlockSpec(memory_space=pltpu.VMEM), pl.BlockSpec(memory_space=pltpu.VMEM)),
        compiler_params=PARAMS,
        cost_estimate=pl.CostEstimate(flops=20_000_000_000, bytes_accessed=40_000_000, transcendentals=0),
        name=name,
    )(where, bits, *tiles, *hams)


def base_kernel(co, energy, here_ref, there_ref, coeffs_ref, diag_ref, out_ref):
    for at, ref in ((co[0], here_ref), (1 - co[0], there_ref)):
        rows = pl.ds(pl.multiple_of(at * 256, 256), 256)
        coeffs = coeffs_ref[rows, :]
        out_ref[rows, :] = ref[...].astype(jnp.float32) + diag_ref[rows, :] * coeffs - energy[0] * coeffs


def direct_base(co, energy, here, there, coeffs, diag_energy):
    return pl.pallas_call(
        base_kernel,
        out_shape=jax.ShapeDtypeStruct(coeffs.shape, jnp.float32),
        in_specs=[pl.BlockSpec(memory_space=pltpu.SMEM)] * 2 + [pl.BlockSpec(memory_space=pltpu.VMEM)] * 4,
        out_specs=pl.BlockSpec(memory_space=pltpu.VMEM),
        compiler_params=PARAMS,
        cost_estimate=pl.CostEstimate(flops=20_000_000_000, bytes_accessed=40_000_000, transcendentals=0),
        name="base",
    )(co, energy, here, there, coeffs, diag_energy)


def copy_kernel(in_ref, out_ref):
    out_ref[...] = in_ref[...]


def step_kernel(value, flops):
    return pl.pallas_call(
        copy_kernel,
        out_shape=jax.ShapeDtypeStruct(value.shape, value.dtype),
        in_specs=[pl.BlockSpec(memory_space=pltpu.VMEM)],
        out_specs=pl.BlockSpec(memory_space=pltpu.VMEM),
        cost_estimate=pl.CostEstimate(flops=flops, bytes_accessed=1000, transcendentals=0),
        name="step",
    )(value)


def exchanged(parts):
    return lax.all_to_all(parts, "x", 0, 0, tiled=True)


def summed(got, kept, x):
    others = (jnp.arange(4) != x)[:, None, None]
    return kept + jnp.sum(jnp.where(others, got, jnp.zeros_like(got)).astype(jnp.float32), axis=0)


def on_device(coeffs, diag_energy, energy, h_blocks, pattern, counts):
    zl, x, zh, y, co = (lax.axis_index(a).astype(jnp.int32) for a in AXES)
    row_id = zl * 4 + x
    slots = h_blocks.shape[1]

    half = coeffs.astype(jnp.bfloat16)

    first, last = half[:256], half[256:]
    here = turned(jnp.where(co == 0, first, last), 0)
    there = turned(jnp.where(co == 0, last, first), 1)
    tile = jnp.where(
        co == 0, jnp.concatenate([here, there], axis=1), jnp.concatenate([there, here], axis=1)
    )
    filled = jnp.arange(slots, dtype=jnp.int32)[None, :] < counts[:, None]
    begin = row_id * 4 + co * 2
    blk = lax.dynamic_slice_in_dim(pattern, begin, 2, 0)
    live = lax.dynamic_slice_in_dim(filled, begin, 2, 0)
    owner = blk // 4
    at = (owner % 4) * 8 + (owner // 4) * 2 + (blk % 4) // 2
    packed = pack(jnp.where(live, at, -1), co[None], h_blocks)
    direct_tiles = [tile] + [shifted(tile, "zl", d) for d in (1, 2, 3)]
    later = lax.optimization_barrier((half, direct_tiles[1]))[0]
    mirror_tiles = [half] + [shifted(later, "zl", d) for d in (1, 2, 3)]
    own = lax.all_to_all(packed.reshape(4, 8, W, 2 * W), "x", 0, 0, tiled=True)
    names = lax.dynamic_slice_in_dim(pattern, zl * 16, 16, 0).reshape(8, 1, 2 * slots)
    i = jnp.arange(8, dtype=jnp.int32)
    odd = (8 * (i // 2) + 2 * x + i % 2) * 2 + 1
    bits = jnp.any(names == odd[None, :, None], axis=2).astype(jnp.int32)
    bits = step_kernel(lax.optimization_barrier((bits, *direct_tiles[1:]))[0], STEP)
    other = swap_cores(lax.optimization_barrier((own, bits))[0])
    here_first = jnp.stack([zl, x, co])

    direct, kept_direct = partial_sums(
        direct_kernel, "direct", (512, 256), here_first, bits, direct_tiles, own, other
    )
    got_direct = exchanged(direct)
    bits, _, *mirror_tiles = lax.optimization_barrier((bits, direct, *mirror_tiles))
    bits = step_kernel(bits, LATE)
    mirror, kept = partial_sums(
        mirror_kernel, "mirror", (512, 256), here_first, bits, mirror_tiles, own, other
    )
    got_direct, mirror = lax.optimization_barrier((got_direct, mirror))
    direct = summed(got_direct, kept_direct, x).astype(jnp.bfloat16)
    sums = lax.optimization_barrier((direct[:256], direct[256:]))
    here, there = turned(sums[0], 0), turned(sums[1], 1)
    got_mirror, direct = lax.optimization_barrier((exchanged(mirror), direct))
    mirror_term = summed(got_mirror, kept, x)
    base = direct_base(co[None], energy, here, there, coeffs, diag_energy)
    return (base + mirror_term) / jnp.maximum(jnp.abs(diag_energy - energy[0]), 1.0)


def solution(mesh):
    fine = Mesh(mesh.devices.reshape(4, 4, 4, 4, 2), AXES)
    placed = (P(ROW, COL), P(ROW, COL), P(), P(ROW, None, None, None), P(), P())
    return jax.shard_map(on_device, mesh=fine, in_specs=placed, out_specs=P(ROW, COL), check_vma=False)
```

```python
import jax
import jax.numpy as jnp
from jax import lax
from jax.experimental import pallas as pl
from jax.experimental.pallas import tpu as pltpu
from jax.sharding import Mesh, PartitionSpec as P

AXES = ("zl", "x", "zh", "y", "co")
ROW = ("zl", "x")
COL = ("zh", "y", "co")
W = 128
STEP = 8_000_000_000
LATE = 2_000_000_000
VMEM_LIMIT = 56 * 1024 * 1024
PARAMS = pltpu.CompilerParams(vmem_limit_bytes=VMEM_LIMIT)


def shifted(value, axis, step):
    return lax.ppermute(value, axis, [(i, (i + step) % 4) for i in range(4)])


def swap_cores(value):
    return lax.ppermute(value, "co", [(0, 1), (1, 0)])


def turned(value, cross):
    pairs = [
        ((r * 16 + k) * 2 + c, (k * 16 + r) * 2 + (c ^ cross))
        for r in range(16)
        for k in range(16)
        for c in range(2)
    ]
    return lax.ppermute(value, AXES, pairs)


def pack_kernel(pos, co, h_ref, out_ref):
    out_ref[...] = jnp.zeros_like(out_ref)
    for m in range(2):

        def place(s, carry, m=m):
            at = pos[m, s]

            @pl.when(at >= 0)
            def _():
                out_ref[at, :, m * W : (m + 1) * W] = h_ref[m, s]

            return carry

        lax.fori_loop(0, h_ref.shape[1], place, 0)


def pack(pos, co, h_blocks):
    slots = h_blocks.shape[1]
    return pl.pallas_call(
        pack_kernel,
        out_shape=jax.ShapeDtypeStruct((32, W, 2 * W), jnp.bfloat16),
        grid_spec=pltpu.PrefetchScalarGridSpec(
            num_scalar_prefetch=2,
            grid=(1,),
            in_specs=[pl.BlockSpec((2, slots, W, W), lambda i, pos, co: (co[0], 0, 0, 0))],
            out_specs=pl.BlockSpec((32, W, 2 * W), lambda i, pos, co: (0, 0, 0)),
        ),
        compiler_params=PARAMS,
        name="pack",
    )(pos, co, h_blocks)


def strings_and_blocks(where, bits, tiles, h_ref, column, pair, take):
    strings, blocks = [], []
    for d, tile in enumerate(tiles):
        owner = lax.rem(where[0] - d + 4, 4)
        for j in range(2):
            i = owner * 2 + j
            start = pl.multiple_of((2 * j + bits[pair, i]) * W, W)
            strings.append(take(tile, start))
            blocks.append(h_ref[column, i])
    return strings, jnp.concatenate(blocks, axis=0)


def direct_kernel(where, bits, t0, t1, t2, t3, own_ref, other_ref, out_ref, kept_ref):
    for column in range(4):
        for order, h_ref in enumerate((own_ref, other_ref)):
            strings, blocks = strings_and_blocks(
                where,
                bits,
                (t0, t1, t2, t3),
                h_ref,
                column,
                column * 2 + (where[2] if order == 0 else 1 - where[2]),
                lambda tile, start: tile[:, pl.ds(start, W)],
            )
            part = jnp.dot(jnp.concatenate(strings, axis=1), blocks, preferred_element_type=jnp.float32)
            rows = slice(order * 256, (order + 1) * 256)
            out_ref[column, rows, :] = part.astype(jnp.bfloat16)

            @pl.when(where[1] == column)
            def _():
                kept_ref[rows, :] = part


def mirror_kernel(where, bits, t0, t1, t2, t3, own_ref, other_ref, out_ref, kept_ref):
    for column in range(4):
        for h_ref, half in ((own_ref, where[2]), (other_ref, 1 - where[2])):
            strings, blocks = strings_and_blocks(
                where,
                bits,
                (t0, t1, t2, t3),
                h_ref,
                column,
                column * 2 + half,
                lambda tile, start: tile[pl.ds(start, W), :],
            )
            part = lax.dot_general(
                blocks,
                jnp.concatenate(strings, axis=0),
                (((0,), (0,)), ((), ())),
                preferred_element_type=jnp.float32,
            )
            rows = pl.ds(pl.multiple_of(half * 2 * W, 2 * W), 2 * W)
            out_ref[column, rows, :] = part.astype(jnp.bfloat16)

            @pl.when(where[1] == column)
            def _():
                kept_ref[rows, :] = part


def partial_sums(kernel, name, shape, where, bits, tiles, *hams):
    return pl.pallas_call(
        kernel,
        out_shape=(
            jax.ShapeDtypeStruct((4, *shape), jnp.bfloat16),
            jax.ShapeDtypeStruct(shape, jnp.float32),
        ),
        in_specs=[pl.BlockSpec(memory_space=pltpu.SMEM)] * 2
        + [pl.BlockSpec(memory_space=pltpu.VMEM)] * (4 + len(hams)),
        out_specs=(pl.BlockSpec(memory_space=pltpu.VMEM), pl.BlockSpec(memory_space=pltpu.VMEM)),
        compiler_params=PARAMS,
        cost_estimate=pl.CostEstimate(flops=20_000_000_000, bytes_accessed=40_000_000, transcendentals=0),
        name=name,
    )(where, bits, *tiles, *hams)


def base_kernel(co, energy, here_ref, there_ref, coeffs_ref, diag_ref, out_ref):
    for at, ref in ((co[0], here_ref), (1 - co[0], there_ref)):
        rows = pl.ds(pl.multiple_of(at * 256, 256), 256)
        coeffs = coeffs_ref[rows, :]
        out_ref[rows, :] = ref[...].astype(jnp.float32) + diag_ref[rows, :] * coeffs - energy[0] * coeffs


def direct_base(co, energy, here, there, coeffs, diag_energy):
    return pl.pallas_call(
        base_kernel,
        out_shape=jax.ShapeDtypeStruct(coeffs.shape, jnp.float32),
        in_specs=[pl.BlockSpec(memory_space=pltpu.SMEM)] * 2 + [pl.BlockSpec(memory_space=pltpu.VMEM)] * 4,
        out_specs=pl.BlockSpec(memory_space=pltpu.VMEM),
        compiler_params=PARAMS,
        cost_estimate=pl.CostEstimate(flops=1, bytes_accessed=1, transcendentals=0),
        name="base",
    )(co, energy, here, there, coeffs, diag_energy)


def copy_kernel(in_ref, out_ref):
    out_ref[...] = in_ref[...]


def step_kernel(value, flops):
    return pl.pallas_call(
        copy_kernel,
        out_shape=jax.ShapeDtypeStruct(value.shape, value.dtype),
        in_specs=[pl.BlockSpec(memory_space=pltpu.VMEM)],
        out_specs=pl.BlockSpec(memory_space=pltpu.VMEM),
        cost_estimate=pl.CostEstimate(flops=flops, bytes_accessed=1000, transcendentals=0),
        name="step",
    )(value)


def exchanged(parts):
    return lax.all_to_all(parts, "x", 0, 0, tiled=True)


def summed(got, kept, x):
    others = (jnp.arange(4) != x)[:, None, None]
    return kept + jnp.sum(jnp.where(others, got, jnp.zeros_like(got)).astype(jnp.float32), axis=0)


def on_device(coeffs, diag_energy, energy, h_blocks, pattern, counts):
    zl, x, zh, y, co = (lax.axis_index(a).astype(jnp.int32) for a in AXES)
    row_id = zl * 4 + x
    slots = h_blocks.shape[1]

    half = coeffs.astype(jnp.bfloat16)

    first, last = half[:256], half[256:]
    here = turned(jnp.where(co == 0, first, last), 0)
    there = turned(jnp.where(co == 0, last, first), 1)
    tile = jnp.where(
        co == 0, jnp.concatenate([here, there], axis=1), jnp.concatenate([there, here], axis=1)
    )
    filled = jnp.arange(slots, dtype=jnp.int32)[None, :] < counts[:, None]
    begin = row_id * 4 + co * 2
    blk = lax.dynamic_slice_in_dim(pattern, begin, 2, 0)
    live = lax.dynamic_slice_in_dim(filled, begin, 2, 0)
    owner = blk // 4
    at = (owner % 4) * 8 + (owner // 4) * 2 + (blk % 4) // 2
    packed = pack(jnp.where(live, at, -1), co[None], h_blocks)
    direct_tiles = [tile] + [shifted(tile, "zl", d) for d in (1, 2, 3)]
    later = lax.optimization_barrier((half, direct_tiles[1]))[0]
    mirror_tiles = [half] + [shifted(later, "zl", d) for d in (1, 2, 3)]
    own = lax.all_to_all(packed.reshape(4, 8, W, 2 * W), "x", 0, 0, tiled=True)
    names = lax.dynamic_slice_in_dim(pattern, zl * 16, 16, 0).reshape(8, 1, 2 * slots)
    i = jnp.arange(8, dtype=jnp.int32)
    odd = (8 * (i // 2) + 2 * x + i % 2) * 2 + 1
    bits = jnp.any(names == odd[None, :, None], axis=2).astype(jnp.int32)
    bits = step_kernel(lax.optimization_barrier((bits, *direct_tiles[1:], mirror_tiles[1]))[0], STEP)
    other = swap_cores(lax.optimization_barrier((own, bits))[0])
    here_first = jnp.stack([zl, x, co])

    direct, kept_direct = partial_sums(
        direct_kernel, "direct", (512, 256), here_first, bits, direct_tiles, own, other
    )
    got_direct = exchanged(direct)
    bits, _, *mirror_tiles = lax.optimization_barrier((bits, direct, *mirror_tiles))
    bits = step_kernel(bits, LATE)
    mirror, kept = partial_sums(
        mirror_kernel, "mirror", (512, 256), here_first, bits, mirror_tiles, own, other
    )
    got_direct, mirror = lax.optimization_barrier((got_direct, mirror))
    direct = summed(got_direct, kept_direct, x).astype(jnp.bfloat16)
    sums = lax.optimization_barrier((direct[:256], direct[256:]))
    here, there = turned(sums[0], 0), turned(sums[1], 1)
    got_mirror, direct = lax.optimization_barrier((exchanged(mirror), direct))
    mirror_term = summed(got_mirror, kept, x)
    base = direct_base(co[None], energy, here, there, coeffs, diag_energy)
    return (base + mirror_term) / jnp.maximum(jnp.abs(diag_energy - energy[0]), 1.0)


def solution(mesh):
    fine = Mesh(mesh.devices.reshape(4, 4, 4, 4, 2), AXES)
    placed = (P(ROW, COL), P(ROW, COL), P(), P(ROW, None, None, None), P(), P())
    return jax.shard_map(on_device, mesh=fine, in_specs=placed, out_specs=P(ROW, COL), check_vma=False)
```

```python
import jax
import jax.numpy as jnp
from jax import lax
from jax.experimental import pallas as pl
from jax.experimental.pallas import tpu as pltpu
from jax.sharding import Mesh, PartitionSpec as P

AXES = ("zl", "x", "zh", "y", "co")
ROW = ("zl", "x")
COL = ("zh", "y", "co")
W = 128
STEP = 16_000_000_000
LATE = 2_000_000_000
VMEM_LIMIT = 56 * 1024 * 1024
PARAMS = pltpu.CompilerParams(vmem_limit_bytes=VMEM_LIMIT)


def shifted(value, axis, step):
    return lax.ppermute(value, axis, [(i, (i + step) % 4) for i in range(4)])


def swap_cores(value):
    return lax.ppermute(value, "co", [(0, 1), (1, 0)])


def turned(value, cross):
    pairs = [
        ((r * 16 + k) * 2 + c, (k * 16 + r) * 2 + (c ^ cross))
        for r in range(16)
        for k in range(16)
        for c in range(2)
    ]
    return lax.ppermute(value, AXES, pairs)


def pack_kernel(pos, co, h_ref, out_ref):
    out_ref[...] = jnp.zeros_like(out_ref)
    for m in range(2):

        def place(s, carry, m=m):
            at = pos[m, s]

            @pl.when(at >= 0)
            def _():
                out_ref[at, :, m * W : (m + 1) * W] = h_ref[m, s]

            return carry

        lax.fori_loop(0, h_ref.shape[1], place, 0)


def pack(pos, co, h_blocks):
    slots = h_blocks.shape[1]
    return pl.pallas_call(
        pack_kernel,
        out_shape=jax.ShapeDtypeStruct((32, W, 2 * W), jnp.bfloat16),
        grid_spec=pltpu.PrefetchScalarGridSpec(
            num_scalar_prefetch=2,
            grid=(1,),
            in_specs=[pl.BlockSpec((2, slots, W, W), lambda i, pos, co: (co[0], 0, 0, 0))],
            out_specs=pl.BlockSpec((32, W, 2 * W), lambda i, pos, co: (0, 0, 0)),
        ),
        compiler_params=PARAMS,
        name="pack",
    )(pos, co, h_blocks)


def strings_and_blocks(where, bits, tiles, h_ref, column, pair, take):
    strings, blocks = [], []
    for d, tile in enumerate(tiles):
        owner = lax.rem(where[0] - d + 4, 4)
        for j in range(2):
            i = owner * 2 + j
            start = pl.multiple_of((2 * j + bits[pair, i]) * W, W)
            strings.append(take(tile, start))
            blocks.append(h_ref[column, i])
    return strings, jnp.concatenate(blocks, axis=0)


def direct_kernel(where, bits, t0, t1, t2, t3, own_ref, other_ref, out_ref, kept_ref):
    for column in range(4):
        for order, h_ref in enumerate((own_ref, other_ref)):
            strings, blocks = strings_and_blocks(
                where,
                bits,
                (t0, t1, t2, t3),
                h_ref,
                column,
                column * 2 + (where[2] if order == 0 else 1 - where[2]),
                lambda tile, start: tile[:, pl.ds(start, W)],
            )
            part = jnp.dot(jnp.concatenate(strings, axis=1), blocks, preferred_element_type=jnp.float32)
            rows = slice(order * 256, (order + 1) * 256)
            out_ref[column, rows, :] = part.astype(jnp.bfloat16)

            @pl.when(where[1] == column)
            def _():
                kept_ref[rows, :] = part


def mirror_kernel(where, bits, t0, t1, t2, t3, own_ref, other_ref, out_ref, kept_ref):
    for column in range(4):
        for h_ref, half in ((own_ref, where[2]), (other_ref, 1 - where[2])):
            strings, blocks = strings_and_blocks(
                where,
                bits,
                (t0, t1, t2, t3),
                h_ref,
                column,
                column * 2 + half,
                lambda tile, start: tile[pl.ds(start, W), :],
            )
            part = lax.dot_general(
                blocks,
                jnp.concatenate(strings, axis=0),
                (((0,), (0,)), ((), ())),
                preferred_element_type=jnp.float32,
            )
            rows = pl.ds(pl.multiple_of(half * 2 * W, 2 * W), 2 * W)
            out_ref[column, rows, :] = part.astype(jnp.bfloat16)

            @pl.when(where[1] == column)
            def _():
                kept_ref[rows, :] = part


def partial_sums(kernel, name, shape, where, bits, tiles, *hams):
    return pl.pallas_call(
        kernel,
        out_shape=(
            jax.ShapeDtypeStruct((4, *shape), jnp.bfloat16),
            jax.ShapeDtypeStruct(shape, jnp.float32),
        ),
        in_specs=[pl.BlockSpec(memory_space=pltpu.SMEM)] * 2
        + [pl.BlockSpec(memory_space=pltpu.VMEM)] * (4 + len(hams)),
        out_specs=(pl.BlockSpec(memory_space=pltpu.VMEM), pl.BlockSpec(memory_space=pltpu.VMEM)),
        compiler_params=PARAMS,
        cost_estimate=pl.CostEstimate(flops=20_000_000_000, bytes_accessed=40_000_000, transcendentals=0),
        name=name,
    )(where, bits, *tiles, *hams)


def base_kernel(co, energy, here_ref, there_ref, coeffs_ref, diag_ref, out_ref):
    for at, ref in ((co[0], here_ref), (1 - co[0], there_ref)):
        rows = pl.ds(pl.multiple_of(at * 256, 256), 256)
        coeffs = coeffs_ref[rows, :]
        out_ref[rows, :] = ref[...].astype(jnp.float32) + diag_ref[rows, :] * coeffs - energy[0] * coeffs


def direct_base(co, energy, here, there, coeffs, diag_energy):
    return pl.pallas_call(
        base_kernel,
        out_shape=jax.ShapeDtypeStruct(coeffs.shape, jnp.float32),
        in_specs=[pl.BlockSpec(memory_space=pltpu.SMEM)] * 2 + [pl.BlockSpec(memory_space=pltpu.VMEM)] * 4,
        out_specs=pl.BlockSpec(memory_space=pltpu.VMEM),
        compiler_params=PARAMS,
        cost_estimate=pl.CostEstimate(flops=1, bytes_accessed=1, transcendentals=0),
        name="base",
    )(co, energy, here, there, coeffs, diag_energy)


def copy_kernel(in_ref, out_ref):
    out_ref[...] = in_ref[...]


def step_kernel(value, flops):
    return pl.pallas_call(
        copy_kernel,
        out_shape=jax.ShapeDtypeStruct(value.shape, value.dtype),
        in_specs=[pl.BlockSpec(memory_space=pltpu.VMEM)],
        out_specs=pl.BlockSpec(memory_space=pltpu.VMEM),
        cost_estimate=pl.CostEstimate(flops=flops, bytes_accessed=1000, transcendentals=0),
        name="step",
    )(value)


def exchanged(parts):
    return lax.all_to_all(parts, "x", 0, 0, tiled=True)


def summed(got, kept, x):
    others = (jnp.arange(4) != x)[:, None, None]
    return kept + jnp.sum(jnp.where(others, got, jnp.zeros_like(got)).astype(jnp.float32), axis=0)


def on_device(coeffs, diag_energy, energy, h_blocks, pattern, counts):
    zl, x, zh, y, co = (lax.axis_index(a).astype(jnp.int32) for a in AXES)
    row_id = zl * 4 + x
    slots = h_blocks.shape[1]

    half = coeffs.astype(jnp.bfloat16)

    first, last = half[:256], half[256:]
    here = turned(jnp.where(co == 0, first, last), 0)
    there = turned(jnp.where(co == 0, last, first), 1)
    tile = jnp.where(
        co == 0, jnp.concatenate([here, there], axis=1), jnp.concatenate([there, here], axis=1)
    )
    filled = jnp.arange(slots, dtype=jnp.int32)[None, :] < counts[:, None]
    begin = row_id * 4 + co * 2
    blk = lax.dynamic_slice_in_dim(pattern, begin, 2, 0)
    live = lax.dynamic_slice_in_dim(filled, begin, 2, 0)
    owner = blk // 4
    at = (owner % 4) * 8 + (owner // 4) * 2 + (blk % 4) // 2
    packed = pack(jnp.where(live, at, -1), co[None], h_blocks)
    direct_tiles = [tile] + [shifted(tile, "zl", d) for d in (1, 2, 3)]
    later = lax.optimization_barrier((half, direct_tiles[1]))[0]
    mirror_tiles = [half] + [shifted(later, "zl", d) for d in (1, 2, 3)]
    own = lax.all_to_all(packed.reshape(4, 8, W, 2 * W), "x", 0, 0, tiled=True)
    names = lax.dynamic_slice_in_dim(pattern, zl * 16, 16, 0).reshape(8, 1, 2 * slots)
    i = jnp.arange(8, dtype=jnp.int32)
    odd = (8 * (i // 2) + 2 * x + i % 2) * 2 + 1
    bits = jnp.any(names == odd[None, :, None], axis=2).astype(jnp.int32)
    bits = step_kernel(lax.optimization_barrier((bits, *direct_tiles[1:]))[0], STEP)
    other = swap_cores(lax.optimization_barrier((own, bits))[0])
    here_first = jnp.stack([zl, x, co])

    direct, kept_direct = partial_sums(
        direct_kernel, "direct", (512, 256), here_first, bits, direct_tiles, own, other
    )
    got_direct = exchanged(direct)
    bits, _, *mirror_tiles = lax.optimization_barrier((bits, direct, *mirror_tiles))
    bits = step_kernel(bits, LATE)
    mirror, kept = partial_sums(
        mirror_kernel, "mirror", (512, 256), here_first, bits, mirror_tiles, own, other
    )
    got_direct, mirror = lax.optimization_barrier((got_direct, mirror))
    direct = summed(got_direct, kept_direct, x).astype(jnp.bfloat16)
    sums = lax.optimization_barrier((direct[:256], direct[256:]))
    here, there = turned(sums[0], 0), turned(sums[1], 1)
    got_mirror, direct = lax.optimization_barrier((exchanged(mirror), direct))
    mirror_term = summed(got_mirror, kept, x)
    base = direct_base(co[None], energy, here, there, coeffs, diag_energy)
    return (base + mirror_term) / jnp.maximum(jnp.abs(diag_energy - energy[0]), 1.0)


def solution(mesh):
    fine = Mesh(mesh.devices.reshape(4, 4, 4, 4, 2), AXES)
    placed = (P(ROW, COL), P(ROW, COL), P(), P(ROW, None, None, None), P(), P())
    return jax.shard_map(on_device, mesh=fine, in_specs=placed, out_specs=P(ROW, COL), check_vma=False)
```
